512 devices in a mesh: gx: 8 (over y, z_hi), gy: 16 (over z_lo, core), sa: 4 (over x).
Axes of the slice: x: 4, y: 4, z: 16 (z_hi: 2, z_lo: 8; z = z_hi * 8 + z_lo), core: 2. Of those that a mesh axis runs over, the one named last changes fastest.
Arguments:
- source: bfloat16 [8, 16, 32, 768], P('gx', 'gy', 'sa'), may hold values from -6 to 6
- group_gain: float32 [4], replicated, may hold values from 0.25 to 4
- shot_group: int32 [32], P('sa'), may hold values from 0 to 3
- block_cols: int32 [8, 16, 32, 4], P('gx', 'gy'), may hold values from 0 to 29, as said below
- block_vals: bfloat16 [8, 16, 32, 4, 128, 128], P('gx', 'gy', 'sa')
Outputs:
- east_out: bfloat16 [8, 16, 32, 1536], P('gx', 'gy', 'sa')
- north_out: bfloat16 [8, 16, 32, 1536], P('gx', 'gy', 'sa')
- interior: bfloat16 [8, 16, 32, 1024], P('gx', 'gy', 'sa')
The draws below stay inside these ranges and needn't reach their ends.
Inputs may be any that keep to these rules, and one draw needn't show every extreme that they name: `block_cols`: in each block row, entry 0 names a west block (6 to 17), entry 1 a south block (18 to 29), the other entries distinct source blocks (below 6).
All inputs are finite; a program needn't handle non-finite values.
Results may differ from the reference program's by a relative error of at most 0.02.
Values may be sent and summed in bfloat16 or wider, within the bound.
A program may use at most 64 MiB of HBM per device.

```python
import math
import jax
import jax.numpy as jnp
from jax import lax

BLK = 128
NT = 12
NS = 6
NU = 8
KB = 4
GROUPS = 4
OUTB = 32
SHOTS = 32
SUBS_X = 8
SUBS_Y = 16


def draw_block_cols(key, part):
    key = jax.random.fold_in(key, 5)
    keys = jax.random.split(key, 4)
    shape = (SUBS_X, SUBS_Y, OUTB)
    west = NS + jax.random.randint(keys[0], shape, 0, NT)
    south = NS + NT + jax.random.randint(keys[1], shape, 0, NT)
    first = jax.random.randint(keys[2], shape, 0, NS)
    second = (first + 1 + jax.random.randint(keys[3], shape, 0, NS - 1)) % NS
    return jnp.stack([west, south, first, second], axis=-1).astype(jnp.int32)


def draw_block_vals(key, part):
    key = jax.random.fold_in(key, 11)
    shape = (SUBS_X, SUBS_Y, OUTB, KB, BLK, BLK)
    slots = jnp.arange(KB)
    shares = jnp.where(slots < 2, 0.45, 0.1 / (KB - 2)).astype(jnp.float32)
    scale = jnp.sqrt(shares / BLK)
    base = jax.random.normal(key, shape, jnp.float32)
    return (base * scale[:, None, None]).astype(jnp.bfloat16)


def set_ends(values, stream_key, least, high):
    extent = values.shape
    place = [jax.random.randint(jax.random.fold_in(stream_key, axis), (), 0, extent[axis]) for axis in range(len(extent))]
    values = values.at[tuple(place)].set(least)
    longest = extent.index(max(extent))
    place[longest] = (place[longest] + 1) % extent[longest]
    return values.at[tuple(place)].set(high)


def levels(rng, shape, cuts, low, largest):
    factor_of, own = 1.0, jax.random.fold_in(rng, 6)
    for axis_at, shards_of in cuts:
        steps = jnp.exp(jax.random.uniform(jax.random.fold_in(own, axis_at), (shards_of,), jnp.float32, low / len(cuts), largest / len(cuts)))
        factor_of = factor_of * jnp.repeat(steps, shape[axis_at] // shards_of).reshape([-1 if axis == axis_at else 1 for axis in range(len(shape))])
    return factor_of


def bell_draw(rng, shape, deviation, bound, pieces=(), dtype=jnp.bfloat16):
    level = levels(rng, shape, pieces, -0.22, 0.18) if pieces else 1.0
    entries = jax.random.normal(rng, shape, jnp.float32) * deviation * level
    return jnp.minimum(jnp.maximum(entries, -bound), bound).astype(dtype)


def setup_inputs(seed: int = 0) -> dict:
    streams_of = jax.random.split(jax.random.key(seed), 6)
    return {
        "source": bell_draw(streams_of[0], (SUBS_X, SUBS_Y, SHOTS, NS * BLK), 1.0, 6.0, ((0, 8), (1, 16), (2, 4))),
        "group_gain": jnp.clip(jnp.exp(jax.random.uniform(streams_of[1], (GROUPS,), jnp.float32, math.log(0.25), math.log(4.0))), 0.25, 4.0),
        "shot_group": set_ends(jax.random.randint(streams_of[2], (SHOTS,), 0, GROUPS), jax.random.fold_in(streams_of[2], 1), 0, GROUPS - 1).astype(jnp.int32),
        "block_cols": draw_block_cols(jax.random.fold_in(streams_of[5], 71), 0),
        "block_vals": draw_block_vals(jax.random.fold_in(streams_of[5], 71), 0),
    }


def solve_blocks(inputs, columns, values):
    stacked = inputs.astype(jnp.float32).reshape(inputs.shape[0], NS + 2 * NT, BLK)
    picked = jnp.take(stacked, columns, axis=1)
    return jnp.einsum("nokc,okcd->nod", picked, values.astype(jnp.float32))


def reference(source, group_gain, shot_group, block_cols, block_vals):
    gains = group_gain[shot_group]
    scaled = (source.astype(jnp.float32) * gains[None, None, :, None]).astype(jnp.bfloat16)
    rows = scaled.shape[2]

    def row_step(east_row, row_data):
        scaled_row, cols_row, vals_row = row_data

        def cell_step(north_in, cell_data):
            scaled_cell, cols_cell, vals_cell, west_in = cell_data
            joined = jnp.concatenate([scaled_cell, west_in, north_in], axis=1)
            result = solve_blocks(joined, cols_cell, vals_cell)
            east_new = result[:, :NT].reshape(rows, NT * BLK).astype(jnp.bfloat16)
            north_new = result[:, NT:2 * NT].reshape(rows, NT * BLK).astype(jnp.bfloat16)
            inner_new = result[:, 2 * NT:].reshape(rows, NU * BLK).astype(jnp.bfloat16)
            return north_new, (east_new, north_new, inner_new)

        start = jnp.zeros((rows, NT * BLK), jnp.bfloat16)
        _, outputs = lax.scan(cell_step, start, (scaled_row, cols_row, vals_row, east_row))
        return outputs[0], outputs

    first = jnp.zeros((SUBS_Y, rows, NT * BLK), jnp.bfloat16)
    _, results = lax.scan(row_step, first, (scaled, block_cols, block_vals))
    return results[0], results[1], results[2]
```

```python
import functools

import jax
import jax.numpy as jnp
from jax import lax
from jax.experimental import pallas as pl
from jax.experimental.pallas import tpu as pltpu
from jax.sharding import PartitionSpec as P

MESH = pl.DeviceIdType.MESH
BLK = 128
NT = 12
NS = 6
OUTB = 32
SA = 4
OWN = OUTB // SA
N = 8


def kernel(nx, ny, source, gain, group, cols, vals, east_out, north_out, inner_out,
           weights, own_src, scaled_all, picked_src, part_send, part, traces, west, south, east, north,
           local_sem, w_send, w_recv, s_send, s_recv, p_send, p_recv, t_send, t_recv):
    gx, gy, sa = lax.axis_index("gx"), lax.axis_index("gy"), lax.axis_index("sa")
    has_west, has_east = gx > 0, gx < nx - 1
    has_south, has_north = gy > 0, gy < ny - 1
    peers = [lax.rem(sa + d, SA) for d in range(SA)]

    barrier = pltpu.get_barrier_semaphore()
    for there, dx, dy in ((has_west, -1, 0), (has_east, 1, 0), (has_south, 0, -1), (has_north, 0, 1)):
        @pl.when(there)
        def _():
            pl.semaphore_signal(barrier, inc=1, device_id=(gx + dx, gy + dy, sa), device_id_type=MESH)
    for d in range(1, SA):
        pl.semaphore_signal(barrier, inc=1, device_id=(gx, gy, peers[d]), device_id_type=MESH)

    own_rows = pl.ds(sa * OWN, OWN)
    src_load = pltpu.make_async_copy(vals.at[:, 2:4], own_src, local_sem)
    src_load.start()

    shot = lax.broadcasted_iota(jnp.int32, (N, BLK), 0)
    gains = jnp.zeros((N, BLK), jnp.float32)
    for s in range(N):
        gains = jnp.where(shot == s, gain[group[s]], gains)
    for pair in range(NS // 2):
        halves = [source[:, (2 * pair + h) * BLK:(2 * pair + h + 1) * BLK].astype(jnp.float32) * gains for h in (0, 1)]
        scaled_all[sa, pair * 16:(pair + 1) * 16, :] = jnp.concatenate(halves, axis=0).astype(jnp.bfloat16)

    neighbours = 3 + sum(there.astype(jnp.int32) for there in (has_west, has_east, has_south, has_north))
    pl.semaphore_wait(barrier, neighbours)

    def scaled_copy(owner, peer):
        return pltpu.make_async_remote_copy(scaled_all.at[owner], scaled_all.at[owner], s_send.at[peer], s_recv.at[owner],
                                            device_id=(gx, gy, peer), device_id_type=MESH)

    def weight_copy(owner, peer):
        rows = pl.ds(owner * OWN, OWN)
        return pltpu.make_async_remote_copy(vals.at[:, 0:2], weights.at[rows], w_send.at[peer], w_recv.at[owner],
                                            device_id=(gx, gy, peer), device_id_type=MESH)

    def part_copy(owner, peer):
        return pltpu.make_async_remote_copy(part_send.at[peer], part.at[owner], p_send.at[peer], p_recv.at[owner],
                                            device_id=(gx, gy, peer), device_id_type=MESH)

    for d in (2, 1, 3):
        scaled_copy(sa, peers[d]).start()
    for d in (2, 1, 3):
        weight_copy(sa, peers[d]).start()
    own_load = pltpu.make_async_copy(vals.at[:, 0:2], weights.at[own_rows], w_recv.at[sa])
    own_load.start()

    for d in (1, 3, 2):
        scaled_copy(peers[d], peers[d]).wait_recv()
    for p in range(SA):
        for pair in range(NS // 2):
            both = scaled_all[p, pair * 16:(pair + 1) * 16, :].astype(jnp.float32)
            picked_src[2 * pair, p * N:(p + 1) * N, :] = both[:N]
            picked_src[2 * pair + 1, p * N:(p + 1) * N, :] = both[N:]
    src_load.wait()
    for r in range(OWN):
        o = sa * OWN + r
        left = jnp.concatenate([picked_src[cols[o, 2]], picked_src[cols[o, 3]]], axis=1).astype(jnp.bfloat16)
        out = jnp.dot(left, own_src[r].reshape(2 * BLK, BLK), preferred_element_type=jnp.float32)
        for p in range(SA):
            part_send[p, r] = out[p * N:(p + 1) * N]
    for d in (2, 1, 3):
        part_copy(sa, peers[d]).start()
    part[sa] = part_send[sa]
    for d in (1, 3, 2):
        part_copy(peers[d], peers[d]).wait_recv()

    def trace_copy(k, src, dst, dx, dy):
        return pltpu.make_async_remote_copy(src, dst, t_send.at[k], t_recv.at[k], device_id=(gx + dx, gy + dy, sa),
                                            device_id_type=MESH)

    east_copy = trace_copy(0, east, west, 1, 0)
    north_copy = trace_copy(1, north, south, 0, 1)

    def arrived(p):
        rows = pl.ds(p * OWN, OWN)
        pltpu.make_async_copy(vals.at[:, 0:2], weights.at[rows], w_recv.at[p]).wait()

    for p in range(SA - 1):
        arrived(p)

    for there, copy, ref, base in ((has_south, north_copy, south, NS + NT), (has_west, east_copy, west, NS)):
        @pl.when(there)
        def _():
            copy.wait_recv()
            for pair in range(NT // 2):
                both = ref[pair * 16:(pair + 1) * 16, :].astype(jnp.float32)
                traces[base + 2 * pair] = both[:N]
                traces[base + 2 * pair + 1] = both[N:]

        @pl.when(jnp.logical_not(there))
        def _():
            for b in range(NT):
                traces[base + b] = jnp.zeros((N, BLK), jnp.float32)

    def row(o):
        left = jnp.concatenate([traces[cols[o, 0]], traces[cols[o, 1]]], axis=1).astype(jnp.bfloat16)
        out = jnp.dot(left, weights[o].reshape(2 * BLK, BLK), preferred_element_type=jnp.float32)
        return out + part[o // OWN, o % OWN]

    for first, ref, there, copy in ((0, east, has_east, east_copy), (NT, north, has_north, north_copy)):
        for pair in range(NT // 2):
            both = jnp.concatenate([row(first + 2 * pair), row(first + 2 * pair + 1)], axis=0)
            ref[pair * 16:(pair + 1) * 16, :] = both.astype(jnp.bfloat16)

        @pl.when(there)
        def _():
            copy.start()

    arrived(SA - 1)
    for o in range(2 * NT, OUTB):
        inner_out[:, (o - 2 * NT) * BLK:(o - 2 * NT + 1) * BLK] = row(o).astype(jnp.bfloat16)
    for ref, out in ((east, east_out), (north, north_out)):
        for pair in range(NT // 2):
            both = ref[pair * 16:(pair + 1) * 16, :]
            out[:, 2 * pair * BLK:(2 * pair + 1) * BLK] = both[:N]
            out[:, (2 * pair + 1) * BLK:(2 * pair + 2) * BLK] = both[N:]

    for d in (1, 2, 3):
        scaled_copy(sa, peers[d]).wait_send()
        weight_copy(sa, peers[d]).wait_send()
        part_copy(sa, peers[d]).wait_send()
    for there, copy in ((has_east, east_copy), (has_north, north_copy)):
        @pl.when(there)
        def _():
            copy.wait_send()


def on_device(nx, ny, source, group_gain, shot_group, block_cols, block_vals):
    vmem, smem = pl.BlockSpec(memory_space=pltpu.VMEM), pl.BlockSpec(memory_space=pltpu.SMEM)
    dma = pltpu.SemaphoreType.DMA
    bf16, f32 = jnp.bfloat16, jnp.float32
    outs = pl.pallas_call(
        functools.partial(kernel, nx, ny),
        out_shape=[jax.ShapeDtypeStruct((N, NT * BLK), bf16), jax.ShapeDtypeStruct((N, NT * BLK), bf16),
                   jax.ShapeDtypeStruct((N, (OUTB - 2 * NT) * BLK), bf16)],
        in_specs=[vmem, smem, smem, smem, pl.BlockSpec(memory_space=pl.ANY)],
        out_specs=[vmem, vmem, vmem],
        scratch_shapes=[
            pltpu.VMEM((OUTB, 2, BLK, BLK), bf16),
            pltpu.VMEM((OWN, 2, BLK, BLK), bf16),
            pltpu.VMEM((SA, NS * N, BLK), bf16),
            pltpu.VMEM((NS, SA * N, BLK), f32),
            pltpu.VMEM((SA, OWN, N, BLK), f32),
            pltpu.VMEM((SA, OWN, N, BLK), f32),
            pltpu.VMEM((NS + 2 * NT, N, BLK), f32),
            pltpu.VMEM((NT * N, BLK), bf16),
            pltpu.VMEM((NT * N, BLK), bf16),
            pltpu.VMEM((NT * N, BLK), bf16),
            pltpu.VMEM((NT * N, BLK), bf16),
            dma, dma((SA,)), dma((SA,)), dma((SA,)), dma((SA,)), dma((SA,)), dma((SA,)), dma((2,)), dma((2,)),
        ],
        compiler_params=pltpu.CompilerParams(collective_id=0, has_side_effects=True, vmem_limit_bytes=40 << 20),
        name="sweep",
    )(source[0, 0], group_gain, shot_group, block_cols[0, 0], block_vals[0, 0])
    return tuple(out[None, None] for out in outs)


def solution(mesh):
    placed = (
        P("gx", "gy", "sa", None),
        P(),
        P("sa"),
        P("gx", "gy", None, None),
        P("gx", "gy", "sa", None, None, None),
    )
    return jax.shard_map(
        functools.partial(on_device, mesh.shape["gx"], mesh.shape["gy"]),
        mesh=mesh,
        in_specs=placed,
        out_specs=(P("gx", "gy", "sa", None), P("gx", "gy", "sa", None), P("gx", "gy", "sa", None)),
        check_vma=False,
    )
```

```python
import functools

import jax
import jax.numpy as jnp
from jax import lax
from jax.experimental import pallas as pl
from jax.experimental.pallas import tpu as pltpu
from jax.sharding import PartitionSpec as P

MESH = pl.DeviceIdType.MESH
BLK = 128
NT = 12
NS = 6
OUTB = 32
SA = 4
OWN = OUTB // SA
N = 8


def kernel(nx, ny, source, gain, group, cols, vals, outs,
           weights, own_src, scaled_all, picked_src, part_send, part, traces, west, south, east, north,
           local_sem, w_send, w_recv, s_send, s_recv, p_send, p_recv, t_send, t_recv):
    gx, gy, sa = lax.axis_index("gx"), lax.axis_index("gy"), lax.axis_index("sa")
    has_west, has_east = gx > 0, gx < nx - 1
    has_south, has_north = gy > 0, gy < ny - 1
    peers = [lax.rem(sa + d, SA) for d in range(SA)]

    barrier = pltpu.get_barrier_semaphore()
    for there, dx, dy in ((has_west, -1, 0), (has_east, 1, 0), (has_south, 0, -1), (has_north, 0, 1)):
        @pl.when(there)
        def _():
            pl.semaphore_signal(barrier, inc=1, device_id=(gx + dx, gy + dy, sa), device_id_type=MESH)
    for d in range(1, SA):
        pl.semaphore_signal(barrier, inc=1, device_id=(gx, gy, peers[d]), device_id_type=MESH)

    src_load = pltpu.make_async_copy(vals.at[:, 2:4], own_src, local_sem)
    src_load.start()

    shot = lax.broadcasted_iota(jnp.int32, (N, BLK), 0)
    gains = jnp.zeros((N, BLK), jnp.float32)
    for s in range(N):
        gains = jnp.where(shot == s, gain[group[s]], gains)
    for pair in range(NS // 2):
        halves = [source[:, (2 * pair + h) * BLK:(2 * pair + h + 1) * BLK].astype(jnp.float32) * gains for h in (0, 1)]
        scaled_all[sa, pair * 16:(pair + 1) * 16, :] = jnp.concatenate(halves, axis=0).astype(jnp.bfloat16)

    neighbours = 3 + sum(there.astype(jnp.int32) for there in (has_west, has_east, has_south, has_north))
    pl.semaphore_wait(barrier, neighbours)

    def scaled_copy(owner, peer):
        return pltpu.make_async_remote_copy(scaled_all.at[owner], scaled_all.at[owner], s_send.at[peer], s_recv.at[owner],
                                            device_id=(gx, gy, peer), device_id_type=MESH)

    def weight_copy(k, owner, peer):
        rows = pl.ds(owner * OWN, OWN)
        return pltpu.make_async_remote_copy(vals.at[:, k:k + 1], weights.at[rows, k:k + 1], w_send.at[k, peer],
                                            w_recv.at[k, owner], device_id=(gx, gy, peer), device_id_type=MESH)

    def own_copy(k, p):
        rows = pl.ds(p * OWN, OWN)
        return pltpu.make_async_copy(vals.at[:, k:k + 1], weights.at[rows, k:k + 1], w_recv.at[k, p])

    needed = (has_west, has_south)

    def send_weights():
        for k in (1, 0):
            @pl.when(needed[k])
            def _():
                for d in (2, 1, 3):
                    weight_copy(k, sa, peers[d]).start()

    def arrived(p):
        for k in (1, 0):
            @pl.when(needed[k])
            def _():
                own_copy(k, p).wait()

    def part_copy(owner, peer):
        return pltpu.make_async_remote_copy(part_send.at[peer], part.at[owner], p_send.at[peer], p_recv.at[owner],
                                            device_id=(gx, gy, peer), device_id_type=MESH)

    for d in (2, 1, 3):
        scaled_copy(sa, peers[d]).start()

    for d in (1, 3, 2):
        scaled_copy(peers[d], peers[d]).wait_recv()
    for p in range(SA):
        for pair in range(NS // 2):
            both = scaled_all[p, pair * 16:(pair + 1) * 16, :].astype(jnp.float32)
            picked_src[2 * pair, p * N:(p + 1) * N, :] = both[:N]
            picked_src[2 * pair + 1, p * N:(p + 1) * N, :] = both[N:]
    src_load.wait()
    for r in range(OWN):
        o = sa * OWN + r
        left = jnp.concatenate([picked_src[cols[2, o]], picked_src[cols[3, o]]], axis=1).astype(jnp.bfloat16)
        out = jnp.dot(left, own_src[r].reshape(2 * BLK, BLK), preferred_element_type=jnp.float32)
        for p in range(SA):
            part_send[p, r] = out[p * N:(p + 1) * N]
    for d in (2, 1, 3):
        part_copy(sa, peers[d]).start()
    pl.when(sa < SA - 1)(send_weights)
    for k in (1, 0):
        @pl.when(needed[k])
        def _():
            own_copy(k, sa).start()

        @pl.when(jnp.logical_not(needed[k]))
        def _():
            weights[:, k] = jnp.zeros((OUTB, BLK, BLK), jnp.bfloat16)
    part[sa] = part_send[sa]
    for d in (1, 3, 2):
        part_copy(peers[d], peers[d]).wait_recv()

    def trace_copy(k, src, dst, dx, dy):
        return pltpu.make_async_remote_copy(src, dst, t_send.at[k], t_recv.at[k], device_id=(gx + dx, gy + dy, sa),
                                            device_id_type=MESH)

    east_copy = trace_copy(0, east, west, 1, 0)
    north_copy = trace_copy(1, north, south, 0, 1)

    for p in range(SA - 1):
        arrived(p)
    pl.when(sa == SA - 1)(send_weights)

    for there, copy, ref, base in ((has_south, north_copy, south, NS + NT), (has_west, east_copy, west, NS)):
        @pl.when(there)
        def _():
            copy.wait_recv()
            for pair in range(NT // 2):
                both = ref[pair * 16:(pair + 1) * 16, :].astype(jnp.float32)
                traces[base + 2 * pair] = both[:N]
                traces[base + 2 * pair + 1] = both[N:]

        @pl.when(jnp.logical_not(there))
        def _():
            for b in range(NT):
                traces[base + b] = jnp.zeros((N, BLK), jnp.float32)

    def row(o):
        left = jnp.concatenate([traces[cols[0, o]], traces[cols[1, o]]], axis=1).astype(jnp.bfloat16)
        out = jnp.dot(left, weights[o].reshape(2 * BLK, BLK), preferred_element_type=jnp.float32)
        return out + part[o // OWN, o % OWN]

    for first, ref, there, copy in ((0, east, has_east, east_copy), (NT, north, has_north, north_copy)):
        for pair in range(NT // 2):
            both = jnp.concatenate([row(first + 2 * pair), row(first + 2 * pair + 1)], axis=0)
            ref[pair * 16:(pair + 1) * 16, :] = both.astype(jnp.bfloat16)

        @pl.when(there)
        def _():
            copy.start()

    arrived(SA - 1)
    for o in range(2 * NT, OUTB):
        outs[:, o * BLK:(o + 1) * BLK] = row(o).astype(jnp.bfloat16)
    for ref, base in ((east, 0), (north, NT)):
        for pair in range(NT // 2):
            both = ref[pair * 16:(pair + 1) * 16, :]
            outs[:, (base + 2 * pair) * BLK:(base + 2 * pair + 1) * BLK] = both[:N]
            outs[:, (base + 2 * pair + 1) * BLK:(base + 2 * pair + 2) * BLK] = both[N:]

    for d in (1, 2, 3):
        scaled_copy(sa, peers[d]).wait_send()
        for k in (0, 1):
            @pl.when(needed[k])
            def _():
                weight_copy(k, sa, peers[d]).wait_send()
        part_copy(sa, peers[d]).wait_send()
    for there, copy in ((has_east, east_copy), (has_north, north_copy)):
        @pl.when(there)
        def _():
            copy.wait_send()


def on_device(nx, ny, source, group_gain, shot_group, block_cols, block_vals):
    vmem, smem = pl.BlockSpec(memory_space=pltpu.VMEM), pl.BlockSpec(memory_space=pltpu.SMEM)
    dma = pltpu.SemaphoreType.DMA
    bf16, f32 = jnp.bfloat16, jnp.float32
    outs = pl.pallas_call(
        functools.partial(kernel, nx, ny),
        out_shape=jax.ShapeDtypeStruct((N, OUTB * BLK), bf16),
        in_specs=[vmem, smem, smem, smem, pl.BlockSpec(memory_space=pl.ANY)],
        out_specs=vmem,
        scratch_shapes=[
            pltpu.VMEM((OUTB, 2, BLK, BLK), bf16),
            pltpu.VMEM((OWN, 2, BLK, BLK), bf16),
            pltpu.VMEM((SA, NS * N, BLK), bf16),
            pltpu.VMEM((NS, SA * N, BLK), f32),
            pltpu.VMEM((SA, OWN, N, BLK), f32),
            pltpu.VMEM((SA, OWN, N, BLK), f32),
            pltpu.VMEM((NS + 2 * NT, N, BLK), f32),
            pltpu.VMEM((NT * N, BLK), bf16),
            pltpu.VMEM((NT * N, BLK), bf16),
            pltpu.VMEM((NT * N, BLK), bf16),
            pltpu.VMEM((NT * N, BLK), bf16),
            dma, dma((2, SA)), dma((2, SA)), dma((SA,)), dma((SA,)), dma((SA,)), dma((SA,)), dma((2,)), dma((2,)),
        ],
        compiler_params=pltpu.CompilerParams(collective_id=0, has_side_effects=True, vmem_limit_bytes=63 << 20),
        name="sweep",
    )(source[0, 0], group_gain, shot_group, block_cols[0, 0].T, block_vals[0, 0])
    outs = outs[None, None]
    return outs[..., :NT * BLK], outs[..., NT * BLK:2 * NT * BLK], outs[..., 2 * NT * BLK:]


def solution(mesh):
    placed = (
        P("gx", "gy", "sa", None),
        P(),
        P("sa"),
        P("gx", "gy", None, None),
        P("gx", "gy", "sa", None, None, None),
    )
    return jax.shard_map(
        functools.partial(on_device, mesh.shape["gx"], mesh.shape["gy"]),
        mesh=mesh,
        in_specs=placed,
        out_specs=(P("gx", "gy", "sa", None), P("gx", "gy", "sa", None), P("gx", "gy", "sa", None)),
        check_vma=False,
    )
```

```python
import functools

import jax
import jax.numpy as jnp
from jax import lax
from jax.experimental import pallas as pl
from jax.experimental.pallas import tpu as pltpu
from jax.sharding import PartitionSpec as P

MESH = pl.DeviceIdType.MESH
BLK = 128
NT = 12
NS = 6
OUTB = 32
SA = 4
OWN = OUTB // SA
N = 8
TRACED = 2 * NT
SENT = TRACED // SA


def sent_slot(o):
    owner, r = divmod(o, OWN)
    return (owner, r) if r < SENT else (SA - 1, (OWN - SENT) * owner + r - SENT)


def kernel(nx, ny, source, gain, group, cols, cols_hbm, vals, east_out, north_out, inner_out,
           weights, own_src, scaled_all, picked_src, part_send, part, traces, west, south, east, north,
           moved, stage, part_moved, part_e, cols_vmem, cols_e, traces_e, west_e, south_e, east_e, north_e,
           local_sem, w_send, w_recv, s_send, s_recv, p_send, p_recv, t_send, t_recv,
           h_send, h_recv, z_send, e_recv, m_send, m_recv, go_sem):
    gx, gy, sa = lax.axis_index("gx"), lax.axis_index("gy"), lax.axis_index("sa")
    odd = lax.rem(gx, 2)
    z = gy // 2
    peers = [lax.rem(sa + d, SA) for d in range(SA)]
    donor = (odd == 0) & (gx > 1)
    host = (odd == 1) & (gx > 1)
    works = jnp.logical_not(donor)
    has_west, has_south, has_north = gx > 0, gy > 0, gy < ny - 1
    z_odd = lax.rem(z, 2) == 1
    chained = donor & z_odd

    barrier = pltpu.get_barrier_semaphore()
    contacts = (
        (odd == 0, 1, 0), (odd == 1, -1, 0), ((odd == 1) & (gx < nx - 1), 2, 0), (host, -2, 0),
        (works & has_south, 0, -1), (works & has_north, 0, 1),
        (chained & (gy >= 4), 0, -4), (chained & (gy < ny - 4), 0, 4),
    )
    for there, dx, dy in contacts:
        @pl.when(there)
        def _():
            pl.semaphore_signal(barrier, inc=1, device_id=(gx + dx, gy + dy, sa), device_id_type=MESH)
    for d in range(1, SA):
        pl.semaphore_signal(barrier, inc=1, device_id=(gx, gy, peers[d]), device_id_type=MESH)

    src_load = pltpu.make_async_copy(vals.at[:, 2:4], own_src, local_sem)
    src_load.start()

    shot = lax.broadcasted_iota(jnp.int32, (N, BLK), 0)
    gains = jnp.zeros((N, BLK), jnp.float32)
    for s in range(N):
        gains = jnp.where(shot == s, gain[group[s]], gains)
    for pair in range(NS // 2):
        halves = [source[:, (2 * pair + h) * BLK:(2 * pair + h + 1) * BLK].astype(jnp.float32) * gains for h in (0, 1)]
        scaled_all[sa, pair * 16:(pair + 1) * 16, :] = jnp.concatenate(halves, axis=0).astype(jnp.bfloat16)

    pl.semaphore_wait(barrier, 3 + sum(there.astype(jnp.int32) for there, _, _ in contacts))

    def copy(src, dst, send, recv, dx=0, dy=0, to=None):
        return pltpu.make_async_remote_copy(src, dst, send, recv, device_id=(gx + dx, gy + dy, sa if to is None else to),
                                            device_id_type=MESH)

    def scaled_copy(owner, peer):
        return copy(scaled_all.at[owner], scaled_all.at[owner], s_send.at[peer], s_recv.at[owner], to=peer)

    def part_copy(owner, peer):
        return copy(part_send.at[peer], part.at[owner], p_send.at[peer], p_recv.at[owner], to=peer)

    def weight_copy(k, owner, peer):
        rows = pl.ds(owner * OWN, OWN)
        return copy(vals.at[:, k:k + 1], weights.at[rows, k:k + 1], w_send.at[k, peer], w_recv.at[k, owner], to=peer)

    def own_copy(k, p):
        rows = pl.ds(p * OWN, OWN)
        return pltpu.make_async_copy(vals.at[:, k:k + 1], weights.at[rows, k:k + 1], w_recv.at[k, p])

    needed = (has_west, has_south)

    def send_weights():
        for k in (1, 0):
            @pl.when(needed[k])
            def _():
                for d in (2, 1, 3):
                    weight_copy(k, sa, peers[d]).start()

    def arrived(p):
        for k in (1, 0):
            @pl.when(needed[k])
            def _():
                own_copy(k, p).wait()

    def shuffle_copy(owner):
        lot = OWN - SENT
        return copy(vals.at[pl.ds(SENT, lot), 0:2], stage.at[pl.ds(owner * lot, lot)], h_send, h_recv.at[owner], to=SA - 1)

    def move_copy(k, last):
        src = stage.at[:, k] if last else vals.at[pl.ds(0, SENT), k]
        return copy(src, moved.at[sa, k], z_send.at[k], m_recv.at[k, sa], dx=1)

    def moved_copy(k, owner, peer):
        return copy(moved.at[owner, k], moved.at[owner, k], m_send.at[k, peer], m_recv.at[k, owner], to=peer)

    part_move = copy(part_moved, part_e, z_send.at[2], e_recv.at[0], dx=1)
    cols_move = copy(cols_hbm, cols_vmem, z_send.at[3], e_recv.at[1], dx=1)

    def moves(act):
        @pl.when(sa < SA - 1)
        def _():
            act(move_copy(0, False))
            pl.when(has_south)(lambda: act(move_copy(1, False)))

        @pl.when(sa == SA - 1)
        def _():
            act(move_copy(0, True))
            pl.when(has_south)(lambda: act(move_copy(1, True)))

    def start_moves():
        @pl.when(sa == SA - 1)
        def _():
            for owner in range(SA - 1):
                shuffle_copy(owner).wait_recv()
        moves(lambda c: c.start())

    for d in (2, 1, 3):
        scaled_copy(sa, peers[d]).start()

    @pl.when(donor)
    def _():
        cols_move.start()
        pl.when(sa < SA - 1)(lambda: shuffle_copy(sa).start())
    early = donor & (jnp.logical_not(z_odd) | (z == 1))
    late = donor & z_odd & (z > 1)
    pl.when(early & (sa < SA - 1))(start_moves)

    for d in (1, 3, 2):
        scaled_copy(peers[d], peers[d]).wait_recv()
    for p in range(SA):
        for pair in range(NS // 2):
            both = scaled_all[p, pair * 16:(pair + 1) * 16, :].astype(jnp.float32)
            picked_src[2 * pair, p * N:(p + 1) * N, :] = both[:N]
            picked_src[2 * pair + 1, p * N:(p + 1) * N, :] = both[N:]
    src_load.wait()
    for r in range(OWN):
        o = sa * OWN + r
        left = jnp.concatenate([picked_src[cols[2, o]], picked_src[cols[3, o]]], axis=1).astype(jnp.bfloat16)
        out = jnp.dot(left, own_src[r].reshape(2 * BLK, BLK), preferred_element_type=jnp.float32)
        for p in range(SA):
            part_send[p, r] = out[p * N:(p + 1) * N]
    for d in (2, 1, 3):
        part_copy(sa, peers[d]).start()
    pl.when(early & (sa == SA - 1))(start_moves)

    pl.when(works & (sa < SA - 1))(send_weights)
    gathers = works | (sa == SA - 1)
    for k in (1, 0):
        @pl.when(needed[k] & gathers)
        def _():
            own_copy(k, sa).start()

        @pl.when(jnp.logical_not(needed[k]))
        def _():
            weights[:, k] = jnp.zeros((OUTB, BLK, BLK), jnp.bfloat16)
    part[sa] = part_send[sa]
    for d in (1, 3, 2):
        part_copy(peers[d], peers[d]).wait_recv()

    def unpack(ref, dst, base):
        for pair in range(NT // 2):
            both = ref[pair * 16:(pair + 1) * 16, :].astype(jnp.float32)
            dst[base + 2 * pair] = both[:N]
            dst[base + 2 * pair + 1] = both[N:]

    def clear(dst, base):
        for b in range(NT):
            dst[base + b] = jnp.zeros((N, BLK), jnp.float32)

    def row(o):
        left = jnp.concatenate([traces[cols[0, o]], traces[cols[1, o]]], axis=1).astype(jnp.bfloat16)
        out = jnp.dot(left, weights[o].reshape(2 * BLK, BLK), preferred_element_type=jnp.float32)
        return out + part[o // OWN, o % OWN]

    def row_e(o):
        left = jnp.concatenate([traces_e[cols_e[0, o]], traces_e[cols_e[1, o]]], axis=1).astype(jnp.bfloat16)
        p, r = sent_slot(o)
        blocks = jnp.concatenate([moved[p, 0, r], moved[p, 1, r]], axis=0)
        return jnp.dot(left, blocks, preferred_element_type=jnp.float32)

    def interior():
        for o in range(TRACED, OUTB):
            inner_out[:, (o - TRACED) * BLK:(o - TRACED + 1) * BLK] = row(o).astype(jnp.bfloat16)

    def put_out():
        for ref, out in ((east, east_out), (north, north_out)):
            for pair in range(NT // 2):
                both = ref[pair * 16:(pair + 1) * 16, :]
                out[:, 2 * pair * BLK:(2 * pair + 1) * BLK] = both[:N]
                out[:, (2 * pair + 1) * BLK:(2 * pair + 2) * BLK] = both[N:]

    west_copy = copy(east, west, t_send.at[0], t_recv.at[0], dx=1)
    west_e_copy = copy(east, west_e, t_send.at[0], t_recv.at[2], dx=2)
    south_copy = copy(north, south, t_send.at[1], t_recv.at[1], dy=1)
    south_e_copy = copy(north_e, south_e, t_send.at[2], t_recv.at[3], dy=1)
    back_west = copy(west_e, west, t_send.at[3], t_recv.at[0], dx=-1)
    back_south = copy(south_e, south, t_send.at[4], t_recv.at[1], dx=-1)
    back_east = copy(east_e, east, t_send.at[5], t_recv.at[4], dx=-1)
    back_north = copy(north_e, north, t_send.at[6], t_recv.at[5], dx=-1)

    @pl.when(donor)
    def _():
        for o in range(0, TRACED, 2):
            both = jnp.concatenate([part[o // OWN, o % OWN], part[o // OWN, o % OWN + 1]], axis=0)
            part_moved[o * N:(o + 2) * N, :] = both.astype(jnp.bfloat16)

        @pl.when(late)
        def _():
            pl.semaphore_wait(go_sem, 1)
            start_moves()
        part_move.start()
        moves(lambda c: c.wait_send())
        part_move.wait_send()

        @pl.when(chained & (gy < ny - 4))
        def _():
            pl.semaphore_signal(go_sem, inc=1, device_id=(gx, gy + 4, sa), device_id_type=MESH)
        pl.when(sa == SA - 1)(send_weights)
        arrived(SA - 1)
        back_west.wait_recv()
        unpack(west, traces, NS)

        @pl.when(has_south)
        def _():
            back_south.wait_recv()
            unpack(south, traces, NS + NT)
        pl.when(jnp.logical_not(has_south))(lambda: clear(traces, NS + NT))
        interior()
        back_east.wait_recv()
        back_north.wait_recv()
        put_out()
        cols_move.wait_send()
        pl.when(sa < SA - 1)(lambda: shuffle_copy(sa).wait_send())

        @pl.when(sa == SA - 1)
        def _():
            for k in (0, 1):
                @pl.when(needed[k])
                def _():
                    for d in (1, 2, 3):
                        weight_copy(k, sa, peers[d]).wait_send()

    @pl.when(host)
    def _():
        @pl.when(jnp.logical_not(has_south))
        def _():
            for p in range(SA):
                moved[p, 1] = jnp.zeros((SENT, BLK, BLK), jnp.bfloat16)
        for k in (0, 1):
            @pl.when(needed[k])
            def _():
                moved_copy(k, sa, peers[1]).wait_recv()
                for d in (2, 1, 3):
                    moved_copy(k, sa, peers[d]).start()

    @pl.when(works)
    def _():
        for p in range(SA - 1):
            arrived(p)
        pl.when(sa == SA - 1)(send_weights)

    @pl.when(host)
    def _():
        cols_move.wait_recv()
        to_smem = pltpu.make_async_copy(cols_vmem, cols_e, local_sem)
        to_smem.start()
        to_smem.wait()
        part_move.wait_recv()
        for k in (0, 1):
            @pl.when(needed[k])
            def _():
                for d in (1, 3, 2):
                    moved_copy(k, peers[d], sa).wait_recv()

        @pl.when(has_south)
        def _():
            south_e_copy.wait_recv()
            unpack(south_e, traces_e, NS + NT)
        pl.when(jnp.logical_not(has_south))(lambda: clear(traces_e, NS + NT))
        west_e_copy.wait_recv()
        unpack(west_e, traces_e, NS)
        for base, ref in ((NT, north_e), (0, east_e)):
            for o in range(base, base + NT, 2):
                both = jnp.concatenate([row_e(o), row_e(o + 1)], axis=0)
                both = (both + part_e[o * N:(o + 2) * N, :].astype(jnp.float32)).astype(jnp.bfloat16)
                ref[(o - base) * N:(o - base + 2) * N, :] = both
            if base:
                pl.when(has_north)(lambda: south_e_copy.start())
        unpack(east_e, traces, NS)

    @pl.when(works)
    def _():
        @pl.when(gx == 1)
        def _():
            west_copy.wait_recv()
            unpack(west, traces, NS)
        pl.when(gx == 0)(lambda: clear(traces, NS))

        @pl.when(has_south)
        def _():
            south_copy.wait_recv()
            unpack(south, traces, NS + NT)
        pl.when(jnp.logical_not(has_south))(lambda: clear(traces, NS + NT))
        for base, ref in ((0, east), (NT, north)):
            for o in range(base, base + NT, 2):
                both = jnp.concatenate([row(o), row(o + 1)], axis=0)
                ref[(o - base) * N:(o - base + 2) * N, :] = both.astype(jnp.bfloat16)
            if base:
                pl.when(has_north)(lambda: south_copy.start())
            else:
                pl.when(gx == 0)(lambda: west_copy.start())
                pl.when((odd == 1) & (gx < nx - 1))(lambda: west_e_copy.start())

        @pl.when(host)
        def _():
            back_west.start()
            pl.when(has_south)(lambda: back_south.start())
            back_east.start()
            back_north.start()
        arrived(SA - 1)
        interior()
        put_out()
        for d in (1, 2, 3):
            for k in (0, 1):
                @pl.when(needed[k])
                def _():
                    weight_copy(k, sa, peers[d]).wait_send()
        pl.when(has_north)(lambda: south_copy.wait_send())
        pl.when(gx == 0)(lambda: west_copy.wait_send())
        pl.when((odd == 1) & (gx < nx - 1))(lambda: west_e_copy.wait_send())

        @pl.when(host)
        def _():
            for k in (0, 1):
                @pl.when(needed[k])
                def _():
                    for d in (1, 2, 3):
                        moved_copy(k, sa, peers[d]).wait_send()
            pl.when(has_north)(lambda: south_e_copy.wait_send())
            back_west.wait_send()
            pl.when(has_south)(lambda: back_south.wait_send())
            back_east.wait_send()
            back_north.wait_send()

    for d in (1, 2, 3):
        scaled_copy(sa, peers[d]).wait_send()
        part_copy(sa, peers[d]).wait_send()


def on_device(nx, ny, source, group_gain, shot_group, block_cols, block_vals):
    vmem, smem, hbm = (pl.BlockSpec(memory_space=m) for m in (pltpu.VMEM, pltpu.SMEM, pl.ANY))
    dma = pltpu.SemaphoreType.DMA
    bf16, f32 = jnp.bfloat16, jnp.float32
    trace = pltpu.VMEM((NT * N, BLK), bf16)
    cols = block_cols[0, 0].T
    outs = pl.pallas_call(
        functools.partial(kernel, nx, ny),
        out_shape=[jax.ShapeDtypeStruct((N, NT * BLK), bf16), jax.ShapeDtypeStruct((N, NT * BLK), bf16),
                   jax.ShapeDtypeStruct((N, (OUTB - TRACED) * BLK), bf16)],
        in_specs=[vmem, smem, smem, smem, hbm, hbm],
        out_specs=[vmem, vmem, vmem],
        scratch_shapes=[
            pltpu.VMEM((OUTB, 2, BLK, BLK), bf16),
            pltpu.VMEM((OWN, 2, BLK, BLK), bf16),
            pltpu.VMEM((SA, NS * N, BLK), bf16),
            pltpu.VMEM((NS, SA * N, BLK), f32),
            pltpu.VMEM((SA, OWN, N, BLK), f32),
            pltpu.VMEM((SA, OWN, N, BLK), f32),
            pltpu.VMEM((NS + 2 * NT, N, BLK), f32),
            trace, trace, trace, trace,
            pltpu.VMEM((SA, 2, SENT, BLK, BLK), bf16),
            pltpu.VMEM((SENT, 2, BLK, BLK), bf16),
            pltpu.VMEM((TRACED * N, BLK), bf16),
            pltpu.VMEM((TRACED * N, BLK), bf16),
            pltpu.VMEM(cols.shape, jnp.int32),
            pltpu.SMEM(cols.shape, jnp.int32),
            pltpu.VMEM((NS + 2 * NT, N, BLK), f32),
            trace, trace, trace, trace,
            dma, dma((2, SA)), dma((2, SA)), dma((SA,)), dma((SA,)), dma((SA,)), dma((SA,)), dma((7,)), dma((6,)),
            dma, dma((SA - 1,)), dma((4,)), dma((2,)), dma((2, SA)), dma((2, SA)), pltpu.SemaphoreType.REGULAR,
        ],
        compiler_params=pltpu.CompilerParams(collective_id=0, has_side_effects=True, vmem_limit_bytes=63 << 20),
        name="sweep",
    )(source[0, 0], group_gain, shot_group, cols, cols, block_vals[0, 0])
    return tuple(out[None, None] for out in outs)


def solution(mesh):
    placed = (
        P("gx", "gy", "sa", None),
        P(),
        P("sa"),
        P("gx", "gy", None, None),
        P("gx", "gy", "sa", None, None, None),
    )
    return jax.shard_map(
        functools.partial(on_device, mesh.shape["gx"], mesh.shape["gy"]),
        mesh=mesh,
        in_specs=placed,
        out_specs=(P("gx", "gy", "sa", None), P("gx", "gy", "sa", None), P("gx", "gy", "sa", None)),
        check_vma=False,
    )
```

```python
import functools

import jax
import jax.numpy as jnp
from jax import lax
from jax.experimental import pallas as pl
from jax.experimental.pallas import tpu as pltpu
from jax.sharding import PartitionSpec as P

MESH = pl.DeviceIdType.MESH
BLK = 128
NT = 12
NS = 6
OUTB = 32
SA = 4
OWN = OUTB // SA
N = 8
TRACED = 2 * NT
SENT = TRACED // SA

HALF = SENT // 2
CHUNKS = ((0, 0), (0, 1), (1, 0), (1, 1))


def sent_slot(o):
    owner, r = divmod(o, OWN)
    return (owner, r) if r < SENT else (SA - 1, (OWN - SENT) * owner + r - SENT)


def kernel(nx, ny, source, gain, group, cols, cols_hbm, vals_hbm, east_out, north_out, inner_out,
           weights, vals, scaled_all, picked_src, part_send, part, traces, west, south, east, north,
           moved, stage, part_moved, part_m, cols_vmem, cols_m, traces_m, south_m, east_m, north_m,
           local_sem, w_send, w_recv, s_send, s_recv, p_send, p_recv, t_send, t_recv,
           h_send, h_recv, z_send, z_more, e_recv, m_send, m_recv, go_sem, ack_sem):
    gx, gy, sa = lax.axis_index("gx"), lax.axis_index("gy"), lax.axis_index("sa")
    odd = lax.rem(gx, 2)
    z = gy // 2
    peers = [lax.rem(sa + d, SA) for d in range(SA)]
    donor = (odd == 1) & (gx < nx - 1)
    host = (odd == 0) & (gx < nx - 2)
    works = jnp.logical_not(donor)
    ends = gx == nx - 1
    before_end = gx == nx - 2
    has_west, has_south, has_north = gx > 0, gy > 0, gy < ny - 1
    z_odd = lax.rem(z, 2) == 1
    chained = donor & z_odd
    chains = chained & (gy < ny - 4)

    barrier = pltpu.get_barrier_semaphore()
    near = (
        ((odd == 0) & (gx < nx - 2), 2, 0), ((odd == 0) & (gx > 1), -2, 0),
        (works & has_south, 0, -1), (works & has_north, 0, 1),
        (chained & (gy >= 4), 0, -4), (chains, 0, 4),
    )
    for there, dx, dy in ((odd == 0, 1, 0),) + near:
        @pl.when(there)
        def _():
            pl.semaphore_signal(barrier, inc=1, device_id=(gx + dx, gy + dy, sa), device_id_type=MESH)
    for d in range(1, SA):
        pl.semaphore_signal(barrier, inc=1, device_id=(gx, gy, peers[d]), device_id_type=MESH)

    load = pltpu.make_async_copy(vals_hbm, vals, local_sem)
    load.start()

    shot = lax.broadcasted_iota(jnp.int32, (N, BLK), 0)
    gains = jnp.zeros((N, BLK), jnp.float32)
    for s in range(N):
        gains = jnp.where(shot == s, gain[group[s]], gains)
    for pair in range(NS // 2):
        halves = [source[:, (2 * pair + h) * BLK:(2 * pair + h + 1) * BLK].astype(jnp.float32) * gains for h in (0, 1)]
        scaled_all[sa, pair * 16:(pair + 1) * 16, :] = jnp.concatenate(halves, axis=0).astype(jnp.bfloat16)

    load.wait()
    pl.semaphore_wait(barrier, 3 + odd + sum(there.astype(jnp.int32) for there, _, _ in near))

    def copy(src, dst, send, recv, dx=0, dy=0, to=None):
        return pltpu.make_async_remote_copy(src, dst, send, recv, device_id=(gx + dx, gy + dy, sa if to is None else to),
                                            device_id_type=MESH)

    def scaled_copy(owner, peer):
        return copy(scaled_all.at[owner], scaled_all.at[owner], s_send.at[peer], s_recv.at[owner], to=peer)

    def part_copy(owner, peer):
        return copy(part_send.at[peer], part.at[owner], p_send.at[peer], p_recv.at[owner], to=peer)

    def weight_copy(k, owner, peer):
        rows = pl.ds(owner * OWN, OWN)
        return copy(vals.at[:, k:k + 1], weights.at[rows, k:k + 1], w_send.at[k, peer], w_recv.at[k, owner], to=peer)

    def own_copy(k, p):
        rows = pl.ds(p * OWN, OWN)
        return pltpu.make_async_copy(vals.at[:, k:k + 1], weights.at[rows, k:k + 1], w_recv.at[k, p])

    needed = (has_west, has_south)

    def send_weights():
        for k in (1, 0):
            @pl.when(needed[k])
            def _():
                for d in (2, 1, 3):
                    weight_copy(k, sa, peers[d]).start()

    def arrived(p):
        for k in (1, 0):
            @pl.when(needed[k])
            def _():
                own_copy(k, p).wait()

    def shuffle_copy(owner):
        lot = OWN - SENT
        return copy(vals.at[pl.ds(SENT, lot), 0:2], stage.at[pl.ds(owner * lot, lot)], h_send, h_recv.at[owner], to=SA - 1)

    def move_copy(k, h, last):
        rows = pl.ds(h * HALF, HALF)
        src = stage.at[rows, k] if last else vals.at[rows, k]
        return copy(src, moved.at[sa, k, rows], z_send.at[k, h], m_recv.at[k, h, sa], dx=-1)

    def moved_copy(k, h, owner, peer):
        ref = moved.at[owner, k, pl.ds(h * HALF, HALF)]
        return copy(ref, ref, m_send.at[k, h, peer], m_recv.at[k, h, owner], to=peer)

    part_move = copy(part_moved, part_m, z_more.at[0], e_recv.at[0], dx=-1)
    cols_move = copy(cols_hbm, cols_vmem, z_more.at[1], e_recv.at[1], dx=-1)

    def moves(act, chunks):
        for last in (False, True):
            @pl.when((sa == SA - 1) if last else (sa < SA - 1))
            def _():
                for k, h in chunks:
                    pl.when(needed[k])(lambda: act(move_copy(k, h, last)))

    def start_moves():
        moves(lambda c: c.start(), CHUNKS)

    early = donor & (jnp.logical_not(z_odd) | (z == 1))
    late = donor & z_odd & (z > 1)

    @pl.when(donor & (sa < SA - 1))
    def _():
        shuffle_copy(sa).start()
    pl.when(donor)(lambda: cols_move.start())
    pl.when(early & (sa < SA - 1))(start_moves)
    for d in (2, 1, 3):
        scaled_copy(sa, peers[d]).start()
    pl.when(ends)(lambda: pl.semaphore_signal(ack_sem, inc=1, device_id=(gx - 1, gy, sa), device_id_type=MESH))

    @pl.when(donor & (sa == SA - 1))
    def _():
        for owner in range(SA - 1):
            shuffle_copy(owner).wait_recv()
        pl.when(early)(start_moves)

    for d in (1, 3, 2):
        scaled_copy(peers[d], peers[d]).wait_recv()
    for p in range(SA):
        for pair in range(NS // 2):
            both = scaled_all[p, pair * 16:(pair + 1) * 16, :].astype(jnp.float32)
            picked_src[2 * pair, p * N:(p + 1) * N, :] = both[:N]
            picked_src[2 * pair + 1, p * N:(p + 1) * N, :] = both[N:]
    for r in range(OWN):
        o = sa * OWN + r
        left = jnp.concatenate([picked_src[cols[2, o]], picked_src[cols[3, o]]], axis=1).astype(jnp.bfloat16)
        out = jnp.dot(left, vals[r, 2:4].reshape(2 * BLK, BLK), preferred_element_type=jnp.float32)
        for p in range(SA):
            part_send[p, r] = out[p * N:(p + 1) * N]
    for d in (2, 1, 3):
        part_copy(sa, peers[d]).start()

    pl.when(works & (sa < SA - 1))(send_weights)
    gathers = works | (sa == SA - 1)
    for k in (1, 0):
        @pl.when(needed[k] & gathers)
        def _():
            own_copy(k, sa).start()

        @pl.when(jnp.logical_not(needed[k]))
        def _():
            weights[:, k] = jnp.zeros((OUTB, BLK, BLK), jnp.bfloat16)
    part[sa] = part_send[sa]
    for d in (1, 3, 2):
        part_copy(peers[d], peers[d]).wait_recv()

    def unpack(ref, dst, base):
        for pair in range(NT // 2):
            both = ref[pair * 16:(pair + 1) * 16, :].astype(jnp.float32)
            dst[base + 2 * pair] = both[:N]
            dst[base + 2 * pair + 1] = both[N:]

    def clear(dst, base):
        for b in range(NT):
            dst[base + b] = jnp.zeros((N, BLK), jnp.float32)

    def row(o):
        left = jnp.concatenate([traces[cols[0, o]], traces[cols[1, o]]], axis=1).astype(jnp.bfloat16)
        out = jnp.dot(left, weights[o].reshape(2 * BLK, BLK), preferred_element_type=jnp.float32)
        return out + part[o // OWN, o % OWN]

    def row_m(o):
        left = jnp.concatenate([traces_m[cols_m[0, o]], traces_m[cols_m[1, o]]], axis=1).astype(jnp.bfloat16)
        p, r = sent_slot(o)
        blocks = jnp.concatenate([moved[p, 0, r], moved[p, 1, r]], axis=0)
        return jnp.dot(left, blocks, preferred_element_type=jnp.float32)

    def interior():
        for o in range(TRACED, OUTB):
            inner_out[:, (o - TRACED) * BLK:(o - TRACED + 1) * BLK] = row(o).astype(jnp.bfloat16)

    def put_out():
        for ref, out in ((east, east_out), (north, north_out)):
            for pair in range(NT // 2):
                both = ref[pair * 16:(pair + 1) * 16, :]
                out[:, 2 * pair * BLK:(2 * pair + 1) * BLK] = both[:N]
                out[:, (2 * pair + 1) * BLK:(2 * pair + 2) * BLK] = both[N:]

    west_copy = copy(east_m, west, t_send.at[0], t_recv.at[0], dx=2)
    west_end_copy = copy(east, west, t_send.at[0], t_recv.at[0], dx=1)
    south_copy = copy(north, south, t_send.at[1], t_recv.at[1], dy=1)
    south_m_copy = copy(north_m, south_m, t_send.at[2], t_recv.at[2], dy=1)
    back_west = copy(east, west, t_send.at[3], t_recv.at[0], dx=1)
    back_south = copy(south_m, south, t_send.at[4], t_recv.at[1], dx=1)
    back_east = copy(east_m, east, t_send.at[5], t_recv.at[3], dx=1)
    back_north = copy(north_m, north, t_send.at[6], t_recv.at[4], dx=1)

    @pl.when(donor)
    def _():
        for o in range(0, TRACED, 2):
            both = jnp.concatenate([part[o // OWN, o % OWN], part[o // OWN, o % OWN + 1]], axis=0)
            part_moved[o * N:(o + 2) * N, :] = both.astype(jnp.bfloat16)

        @pl.when(late)
        def _():
            pl.semaphore_wait(go_sem, 1)
            start_moves()
        part_move.start()
        moves(lambda c: c.wait_send(), CHUNKS)
        part_move.wait_send()

        @pl.when(chains)
        def _():
            pl.semaphore_signal(go_sem, inc=1, device_id=(gx, gy + 4, sa), device_id_type=MESH)
        pl.when(sa == SA - 1)(send_weights)
        arrived(SA - 1)
        back_west.wait_recv()
        unpack(west, traces, NS)

        @pl.when(has_south)
        def _():
            back_south.wait_recv()
            unpack(south, traces, NS + NT)
        pl.when(jnp.logical_not(has_south))(lambda: clear(traces, NS + NT))
        interior()
        back_east.wait_recv()
        back_north.wait_recv()
        put_out()
        cols_move.wait_send()
        pl.when(sa < SA - 1)(lambda: shuffle_copy(sa).wait_send())

        @pl.when(sa == SA - 1)
        def _():
            for k in (0, 1):
                @pl.when(needed[k])
                def _():
                    for d in (1, 2, 3):
                        weight_copy(k, sa, peers[d]).wait_send()

    @pl.when(works)
    def _():
        for p in range(SA - 1):
            arrived(p)

    needed_m = (gx >= 0, has_south)

    def do_native():
        @pl.when(has_south)
        def _():
            south_copy.wait_recv()
            unpack(south, traces, NS + NT)
        pl.when(jnp.logical_not(has_south))(lambda: clear(traces, NS + NT))
        @pl.when(has_west)
        def _():
            west_copy.wait_recv()
            unpack(west, traces, NS)
        pl.when(jnp.logical_not(has_west))(lambda: clear(traces, NS))
        for base, ref in ((NT, north), (0, east)):
            for o in range(base, base + NT, 2):
                both = jnp.concatenate([row(o), row(o + 1)], axis=0)
                ref[(o - base) * N:(o - base + 2) * N, :] = both.astype(jnp.bfloat16)
            if base:
                pl.when(has_north)(lambda: south_copy.start())

        @pl.when(before_end)
        def _():
            pl.semaphore_wait(ack_sem, 1)
            west_end_copy.start()

    @pl.when(host)
    def _():
        @pl.when(jnp.logical_not(has_south))
        def _():
            for p in range(SA):
                moved[p, 1] = jnp.zeros((SENT, BLK, BLK), jnp.bfloat16)
        for k, h in CHUNKS:
            @pl.when(needed_m[k])
            def _():
                moved_copy(k, h, sa, peers[1]).wait_recv()
                for d in (2, 1, 3):
                    moved_copy(k, h, sa, peers[d]).start()
        cols_move.wait_recv()
        to_smem = pltpu.make_async_copy(cols_vmem, cols_m, local_sem)
        to_smem.start()
        to_smem.wait()
        part_move.wait_recv()
        for k, h in CHUNKS:
            @pl.when(needed_m[k])
            def _():
                for d in (1, 3, 2):
                    moved_copy(k, h, peers[d], sa).wait_recv()

    pl.when(works & (sa == SA - 1))(send_weights)
    pl.when(works)(do_native)

    @pl.when(host)
    def _():
        unpack(east, traces_m, NS)

        @pl.when(has_south)
        def _():
            south_m_copy.wait_recv()
            unpack(south_m, traces_m, NS + NT)
        pl.when(jnp.logical_not(has_south))(lambda: clear(traces_m, NS + NT))
        for base, ref in ((NT, north_m), (0, east_m)):
            for o in range(base, base + NT, 2):
                both = jnp.concatenate([row_m(o), row_m(o + 1)], axis=0)
                both = (both + part_m[o * N:(o + 2) * N, :].astype(jnp.float32)).astype(jnp.bfloat16)
                ref[(o - base) * N:(o - base + 2) * N, :] = both
            if base:
                pl.when(has_north)(lambda: south_m_copy.start())
        west_copy.start()
        back_west.start()
        pl.when(has_south)(lambda: back_south.start())
        back_east.start()
        back_north.start()

    @pl.when(works)
    def _():
        arrived(SA - 1)
        interior()
        put_out()
        for d in (1, 2, 3):
            for k in (0, 1):
                @pl.when(needed[k])
                def _():
                    weight_copy(k, sa, peers[d]).wait_send()
        pl.when(has_north)(lambda: south_copy.wait_send())
        pl.when(before_end)(lambda: west_end_copy.wait_send())

        @pl.when(host)
        def _():
            for k, h in CHUNKS:
                @pl.when(needed_m[k])
                def _():
                    for d in (1, 2, 3):
                        moved_copy(k, h, sa, peers[d]).wait_send()
            pl.when(has_north)(lambda: south_m_copy.wait_send())
            west_copy.wait_send()
            back_west.wait_send()
            pl.when(has_south)(lambda: back_south.wait_send())
            back_east.wait_send()
            back_north.wait_send()

    for d in (1, 2, 3):
        scaled_copy(sa, peers[d]).wait_send()
        part_copy(sa, peers[d]).wait_send()


def on_device(nx, ny, source, group_gain, shot_group, block_cols, block_vals):
    vmem, smem, hbm = (pl.BlockSpec(memory_space=m) for m in (pltpu.VMEM, pltpu.SMEM, pl.ANY))
    dma = pltpu.SemaphoreType.DMA
    bf16, f32 = jnp.bfloat16, jnp.float32
    trace = pltpu.VMEM((NT * N, BLK), bf16)
    cols = block_cols[0, 0].T
    outs = pl.pallas_call(
        functools.partial(kernel, nx, ny),
        out_shape=[jax.ShapeDtypeStruct((N, NT * BLK), bf16), jax.ShapeDtypeStruct((N, NT * BLK), bf16),
                   jax.ShapeDtypeStruct((N, (OUTB - TRACED) * BLK), bf16)],
        in_specs=[vmem, smem, smem, smem, hbm, hbm],
        out_specs=[vmem, vmem, vmem],
        scratch_shapes=[
            pltpu.VMEM((OUTB, 2, BLK, BLK), bf16),
            pltpu.VMEM((OWN, 4, BLK, BLK), bf16),
            pltpu.VMEM((SA, NS * N, BLK), bf16),
            pltpu.VMEM((NS, SA * N, BLK), f32),
            pltpu.VMEM((SA, OWN, N, BLK), f32),
            pltpu.VMEM((SA, OWN, N, BLK), f32),
            pltpu.VMEM((NS + 2 * NT, N, BLK), f32),
            trace, trace, trace, trace,
            pltpu.VMEM((SA, 2, SENT, BLK, BLK), bf16),
            pltpu.VMEM((SENT, 2, BLK, BLK), bf16),
            pltpu.VMEM((TRACED * N, BLK), bf16),
            pltpu.VMEM((TRACED * N, BLK), bf16),
            pltpu.VMEM(cols.shape, jnp.int32),
            pltpu.SMEM(cols.shape, jnp.int32),
            pltpu.VMEM((NS + 2 * NT, N, BLK), f32),
            trace, trace, trace,
            dma, dma((2, SA)), dma((2, SA)), dma((SA,)), dma((SA,)), dma((SA,)), dma((SA,)), dma((7,)), dma((5,)),
            dma, dma((SA - 1,)), dma((2, 2)), dma((2,)), dma((2,)), dma((2, 2, SA)), dma((2, 2, SA)),
            pltpu.SemaphoreType.REGULAR, pltpu.SemaphoreType.REGULAR,
        ],
        compiler_params=pltpu.CompilerParams(collective_id=0, has_side_effects=True, vmem_limit_bytes=63 << 20),
        name="sweep",
    )(source[0, 0], group_gain, shot_group, cols, cols, block_vals[0, 0])
    return tuple(out[None, None] for out in outs)


def solution(mesh):
    placed = (
        P("gx", "gy", "sa", None),
        P(),
        P("sa"),
        P("gx", "gy", None, None),
        P("gx", "gy", "sa", None, None, None),
    )
    return jax.shard_map(
        functools.partial(on_device, mesh.shape["gx"], mesh.shape["gy"]),
        mesh=mesh,
        in_specs=placed,
        out_specs=(P("gx", "gy", "sa", None), P("gx", "gy", "sa", None), P("gx", "gy", "sa", None)),
        check_vma=False,
    )
```

```python
import functools

import jax
import jax.numpy as jnp
from jax import lax
from jax.experimental import pallas as pl
from jax.experimental.pallas import tpu as pltpu
from jax.sharding import PartitionSpec as P

MESH = pl.DeviceIdType.MESH
BLK = 128
NT = 12
NS = 6
OUTB = 32
SA = 4
OWN = OUTB // SA
N = 8
TRACED = 2 * NT
CHUNKS = ((0, 0), (0, 1), (1, 0), (1, 1))
SENT = (6, 7)
LOT = tuple(OWN - sent for sent in SENT)


def piece(k, h, last):
    count = (SA - 1) * LOT[k] if last else SENT[k]
    first = (count + 1) // 2
    return pl.ds(first, count - first) if h else pl.ds(0, first)


def sent_slot(o, k):
    owner, r = divmod(o, OWN)
    return (owner, r) if r < SENT[k] else (SA - 1, LOT[k] * owner + r - SENT[k])


def each(owner, act):
    pl.when(owner < SA - 1)(lambda: act(False))
    pl.when(owner == SA - 1)(lambda: act(True))


def kernel(nx, ny, source, gain, group, cols, cols_hbm, vals_hbm, east_out, north_out, inner_out,
           weights, vals, scaled_all, picked_src, part_send, part, traces, west, south, east, north,
           moved_w, moved_s, stage_w, stage_s, part_moved, part_m, cols_vmem, cols_m, traces_m, south_m, east_m, north_m,
           local_sem, w_send, w_recv, s_send, s_recv, p_send, p_recv, t_send, t_recv,
           h_send, h_recv, z_send, z_more, e_recv, m_send, m_recv, f_send, f_moved, go_sem, ack_sem):
    gx, gy, sa = lax.axis_index("gx"), lax.axis_index("gy"), lax.axis_index("sa")
    moved, stage = (moved_w, moved_s), (stage_w, stage_s)
    odd = lax.rem(gx, 2)
    z = gy // 2
    peers = [lax.rem(sa + d, SA) for d in range(SA)]
    donor = (odd == 1) & (gx < nx - 1)
    host = (odd == 0) & (gx < nx - 2)
    works = jnp.logical_not(donor)
    ends = gx == nx - 1
    before_end = gx == nx - 2
    has_west, has_south, has_north = gx > 0, gy > 0, gy < ny - 1
    z_odd = lax.rem(z, 2) == 1
    chained = donor & z_odd
    chains = chained & (gy < ny - 4)

    barrier = pltpu.get_barrier_semaphore()
    near = (
        ((odd == 0) & (gx < nx - 2), 2, 0), ((odd == 0) & (gx > 1), -2, 0),
        (works & has_south, 0, -1), (works & has_north, 0, 1),
        (chained & (gy >= 4), 0, -4), (chains, 0, 4),
    )
    for there, dx, dy in ((odd == 0, 1, 0),) + near:
        @pl.when(there)
        def _():
            pl.semaphore_signal(barrier, inc=1, device_id=(gx + dx, gy + dy, sa), device_id_type=MESH)
    for d in range(1, SA):
        pl.semaphore_signal(barrier, inc=1, device_id=(gx, gy, peers[d]), device_id_type=MESH)

    load = pltpu.make_async_copy(vals_hbm, vals, local_sem)
    load.start()

    shot = lax.broadcasted_iota(jnp.int32, (N, BLK), 0)
    gains = jnp.zeros((N, BLK), jnp.float32)
    for s in range(N):
        gains = jnp.where(shot == s, gain[group[s]], gains)
    for pair in range(NS // 2):
        halves = [source[:, (2 * pair + h) * BLK:(2 * pair + h + 1) * BLK].astype(jnp.float32) * gains for h in (0, 1)]
        scaled_all[sa, pair * 16:(pair + 1) * 16, :] = jnp.concatenate(halves, axis=0).astype(jnp.bfloat16)

    load.wait()
    pl.semaphore_wait(barrier, 3 + odd + sum(there.astype(jnp.int32) for there, _, _ in near))

    def copy(src, dst, send, recv, dx=0, dy=0, to=None):
        return pltpu.make_async_remote_copy(src, dst, send, recv, device_id=(gx + dx, gy + dy, sa if to is None else to),
                                            device_id_type=MESH)

    def scaled_copy(owner, peer):
        return copy(scaled_all.at[owner], scaled_all.at[owner], s_send.at[peer], s_recv.at[owner], to=peer)

    def part_copy(owner, peer):
        return copy(part_send.at[peer], part.at[owner], p_send.at[peer], p_recv.at[owner], to=peer)

    def weight_copy(k, owner, peer):
        rows = pl.ds(owner * OWN, OWN)
        return copy(vals.at[:, k:k + 1], weights.at[rows, k:k + 1], w_send.at[k, peer], w_recv.at[k, owner], to=peer)

    def own_copy(k, p):
        rows = pl.ds(p * OWN, OWN)
        return pltpu.make_async_copy(vals.at[:, k:k + 1], weights.at[rows, k:k + 1], w_recv.at[k, p])

    needed = (has_west, has_south)

    def weights_do(act, ds):
        for k in (1, 0):
            @pl.when(needed[k])
            def _():
                for d in ds:
                    act(weight_copy(k, sa, peers[d]))

    def send_interior():
        weights_do(lambda c: c.start(), (2, 1, 3))

    def arrived(p):
        for k in (1, 0):
            @pl.when(needed[k])
            def _():
                own_copy(k, p).wait()

    def pass_on(k, d):
        rows = pl.ds(peers[d] * OWN, OWN)
        ref = weights.at[rows, k:k + 1]
        return copy(ref, ref, f_send.at[k], w_recv.at[k, peers[d]], to=peers[SA - d])

    def pass_moved(k, h, last):
        d = 1 if h else SA - 1
        ref = moved[k].at[peers[d], piece(k, h, last)]
        return copy(ref, ref, f_moved.at[k, h], m_recv.at[k, h, peers[d]], to=peers[SA - d])

    def shuffle_copy(k, owner):
        return copy(vals.at[pl.ds(SENT[k], LOT[k]), k], stage[k].at[pl.ds(owner * LOT[k], LOT[k])], h_send.at[k],
                    h_recv.at[k, owner], to=SA - 1)

    def move_copy(k, h, last):
        rows = piece(k, h, last)
        src = stage[k].at[rows] if last else vals.at[rows, k]
        return copy(src, moved[k].at[sa, rows], z_send.at[k, h], m_recv.at[k, h, sa], dx=-1)

    def moved_copy(k, h, owner, peer, last):
        ref = moved[k].at[owner, piece(k, h, last)]
        return copy(ref, ref, m_send.at[k, h, peer], m_recv.at[k, h, owner], to=peer)

    part_move = copy(part_moved, part_m, z_more.at[0], e_recv.at[0], dx=-1)
    cols_move = copy(cols_hbm, cols_vmem, z_more.at[1], e_recv.at[1], dx=-1)

    def moves(act, chunks):
        for last in (False, True):
            @pl.when((sa == SA - 1) if last else (sa < SA - 1))
            def _():
                for k, h in chunks:
                    pl.when(needed[k])(lambda: act(move_copy(k, h, last)))

    def start_moves():
        moves(lambda c: c.start(), CHUNKS)

    early = donor & (jnp.logical_not(z_odd) | (z == 1))
    late = donor & z_odd & (z > 1)

    @pl.when(donor & (sa < SA - 1))
    def _():
        for k in (0, 1):
            shuffle_copy(k, sa).start()
    pl.when(donor)(lambda: cols_move.start())
    pl.when(early & (sa < SA - 1))(start_moves)
    for d in (2, 1, 3):
        scaled_copy(sa, peers[d]).start()
    pl.when(ends)(lambda: pl.semaphore_signal(ack_sem, inc=1, device_id=(gx - 1, gy, sa), device_id_type=MESH))

    @pl.when(donor & (sa == SA - 1))
    def _():
        for owner in range(SA - 1):
            for k in (0, 1):
                shuffle_copy(k, owner).wait_recv()
        pl.when(early)(start_moves)

    for d in (1, 3, 2):
        scaled_copy(peers[d], peers[d]).wait_recv()
    for p in range(SA):
        for pair in range(NS // 2):
            both = scaled_all[p, pair * 16:(pair + 1) * 16, :].astype(jnp.float32)
            picked_src[2 * pair, p * N:(p + 1) * N, :] = both[:N]
            picked_src[2 * pair + 1, p * N:(p + 1) * N, :] = both[N:]
    for r in range(OWN):
        o = sa * OWN + r
        left = jnp.concatenate([picked_src[cols[2, o]], picked_src[cols[3, o]]], axis=1).astype(jnp.bfloat16)
        out = jnp.dot(left, vals[r, 2:4].reshape(2 * BLK, BLK), preferred_element_type=jnp.float32)
        for p in range(SA):
            part_send[p, r] = out[p * N:(p + 1) * N]
    for d in (2, 1, 3):
        part_copy(sa, peers[d]).start()

    pl.when(works & (sa < SA - 1))(lambda: weights_do(lambda c: c.start(), (1, 3)))
    gathers = works | (sa == SA - 1)
    for k in (1, 0):
        @pl.when(needed[k] & gathers)
        def _():
            own_copy(k, sa).start()

        @pl.when(jnp.logical_not(needed[k]))
        def _():
            weights[:, k] = jnp.zeros((OUTB, BLK, BLK), jnp.bfloat16)
    part[sa] = part_send[sa]
    for d in (1, 3, 2):
        part_copy(peers[d], peers[d]).wait_recv()

    def unpack(ref, dst, base):
        for pair in range(NT // 2):
            both = ref[pair * 16:(pair + 1) * 16, :].astype(jnp.float32)
            dst[base + 2 * pair] = both[:N]
            dst[base + 2 * pair + 1] = both[N:]

    def clear(dst, base):
        for b in range(NT):
            dst[base + b] = jnp.zeros((N, BLK), jnp.float32)

    def row(o):
        left = jnp.concatenate([traces[cols[0, o]], traces[cols[1, o]]], axis=1).astype(jnp.bfloat16)
        out = jnp.dot(left, weights[o].reshape(2 * BLK, BLK), preferred_element_type=jnp.float32)
        return out + part[o // OWN, o % OWN]

    def row_m(o):
        left = jnp.concatenate([traces_m[cols_m[0, o]], traces_m[cols_m[1, o]]], axis=1).astype(jnp.bfloat16)
        blocks = jnp.concatenate([moved[k][sent_slot(o, k)] for k in (0, 1)], axis=0)
        return jnp.dot(left, blocks, preferred_element_type=jnp.float32)

    def interior():
        for o in range(TRACED, OUTB):
            inner_out[:, (o - TRACED) * BLK:(o - TRACED + 1) * BLK] = row(o).astype(jnp.bfloat16)

    def put_out():
        for ref, out in ((east, east_out), (north, north_out)):
            for pair in range(NT // 2):
                both = ref[pair * 16:(pair + 1) * 16, :]
                out[:, 2 * pair * BLK:(2 * pair + 1) * BLK] = both[:N]
                out[:, (2 * pair + 1) * BLK:(2 * pair + 2) * BLK] = both[N:]

    west_copy = copy(east_m, west, t_send.at[0], t_recv.at[0], dx=2)
    west_end_copy = copy(east, west, t_send.at[0], t_recv.at[0], dx=1)
    south_copy = copy(north, south, t_send.at[1], t_recv.at[1], dy=1)
    south_m_copy = copy(north_m, south_m, t_send.at[2], t_recv.at[2], dy=1)
    back_west = copy(east, west, t_send.at[3], t_recv.at[0], dx=1)
    back_south = copy(south_m, south, t_send.at[4], t_recv.at[1], dx=1)
    back_east = copy(east_m, east, t_send.at[5], t_recv.at[3], dx=1)
    back_north = copy(north_m, north, t_send.at[6], t_recv.at[4], dx=1)

    @pl.when(donor)
    def _():
        for o in range(0, TRACED, 2):
            both = jnp.concatenate([part[o // OWN, o % OWN], part[o // OWN, o % OWN + 1]], axis=0)
            part_moved[o * N:(o + 2) * N, :] = both.astype(jnp.bfloat16)

        @pl.when(late)
        def _():
            pl.semaphore_wait(go_sem, 1)
            start_moves()
        part_move.start()
        moves(lambda c: c.wait_send(), CHUNKS)
        part_move.wait_send()

        @pl.when(chains)
        def _():
            pl.semaphore_signal(go_sem, inc=1, device_id=(gx, gy + 4, sa), device_id_type=MESH)
        pl.when(sa == SA - 1)(send_interior)
        arrived(SA - 1)
        back_west.wait_recv()
        unpack(west, traces, NS)

        @pl.when(has_south)
        def _():
            back_south.wait_recv()
            unpack(south, traces, NS + NT)
        pl.when(jnp.logical_not(has_south))(lambda: clear(traces, NS + NT))
        interior()
        back_east.wait_recv()
        back_north.wait_recv()
        put_out()
        cols_move.wait_send()
        for k in (0, 1):
            pl.when(sa < SA - 1)(lambda: shuffle_copy(k, sa).wait_send())

        pl.when(sa == SA - 1)(lambda: weights_do(lambda c: c.wait_send(), (1, 2, 3)))

    passes = ((1, 1), (0, 3))

    @pl.when(works)
    def _():
        for k, d in passes:
            @pl.when(needed[k] & (peers[d] < SA - 1))
            def _():
                own_copy(k, peers[d]).wait()
                pass_on(k, d).start()
        for d in range(SA):
            for k in (1, 0):
                if (k, d) not in passes:
                    @pl.when(needed[k] & (peers[d] < SA - 1))
                    def _():
                        own_copy(k, peers[d]).wait()
        pl.when((sa == SA - 1) & ((gx >= nx - 2) | (z >= 4)))(send_interior)

    needed_m = (gx >= 0, has_south)

    def do_native():
        @pl.when(has_south)
        def _():
            south_copy.wait_recv()
            unpack(south, traces, NS + NT)
        pl.when(jnp.logical_not(has_south))(lambda: clear(traces, NS + NT))
        @pl.when(has_west)
        def _():
            west_copy.wait_recv()
            unpack(west, traces, NS)
        pl.when(jnp.logical_not(has_west))(lambda: clear(traces, NS))
        for base, ref in ((NT, north), (0, east)):
            for o in range(base, base + NT, 2):
                both = jnp.concatenate([row(o), row(o + 1)], axis=0)
                ref[(o - base) * N:(o - base + 2) * N, :] = both.astype(jnp.bfloat16)
            if base:
                pl.when(has_north)(lambda: south_copy.start())

        @pl.when(before_end)
        def _():
            pl.semaphore_wait(ack_sem, 1)
            west_end_copy.start()

    @pl.when(host)
    def _():
        @pl.when(jnp.logical_not(has_south))
        def _():
            for p in range(SA):
                moved[1][p] = jnp.zeros((SENT[1], BLK, BLK), jnp.bfloat16)
        for k, h in CHUNKS:
            @pl.when(needed_m[k])
            def _():
                def move_on(last):
                    moved_copy(k, h, sa, peers[1], last).wait_recv()
                    for d in (1, 3):
                        moved_copy(k, h, sa, peers[d], last).start()
                each(sa, move_on)
        for k, h in CHUNKS:
            @pl.when(needed_m[k])
            def _():
                def move_on(last):
                    moved_copy(k, h, peers[1 if h else SA - 1], sa, last).wait_recv()
                    pass_moved(k, h, last).start()
                each(peers[1 if h else SA - 1], move_on)
        cols_move.wait_recv()
        to_smem = pltpu.make_async_copy(cols_vmem, cols_m, local_sem)
        to_smem.start()
        to_smem.wait()
        part_move.wait_recv()
        for k, h in CHUNKS:
            @pl.when(needed_m[k])
            def _():
                for d in (SA - 1 if h else 1, 2):
                    each(peers[d], lambda last: moved_copy(k, h, peers[d], sa, last).wait_recv())

    pl.when(works)(do_native)

    @pl.when(host)
    def _():
        unpack(east, traces_m, NS)

        @pl.when(has_south)
        def _():
            south_m_copy.wait_recv()
            unpack(south_m, traces_m, NS + NT)
        pl.when(jnp.logical_not(has_south))(lambda: clear(traces_m, NS + NT))
        for base, ref in ((NT, north_m), (0, east_m)):
            for o in range(base, base + NT, 2):
                both = jnp.concatenate([row_m(o), row_m(o + 1)], axis=0)
                both = (both + part_m[o * N:(o + 2) * N, :].astype(jnp.float32)).astype(jnp.bfloat16)
                ref[(o - base) * N:(o - base + 2) * N, :] = both
            if base:
                pl.when(has_north)(lambda: south_m_copy.start())
        west_copy.start()
        back_west.start()
        pl.when(has_south)(lambda: back_south.start())
        back_east.start()
        back_north.start()
        pl.when((sa == SA - 1) & (z < 4))(send_interior)

    @pl.when(works)
    def _():
        arrived(SA - 1)
        interior()
        put_out()
        pl.when(sa < SA - 1)(lambda: weights_do(lambda c: c.wait_send(), (1, 3)))
        pl.when(sa == SA - 1)(lambda: weights_do(lambda c: c.wait_send(), (1, 2, 3)))
        for k, d in passes:
            pl.when(needed[k] & (peers[d] < SA - 1))(lambda: pass_on(k, d).wait_send())
        pl.when(has_north)(lambda: south_copy.wait_send())
        pl.when(before_end)(lambda: west_end_copy.wait_send())

        @pl.when(host)
        def _():
            for k, h in CHUNKS:
                @pl.when(needed_m[k])
                def _():
                    for d in (1, 3):
                        each(sa, lambda last: moved_copy(k, h, sa, peers[d], last).wait_send())
                    each(peers[1 if h else SA - 1], lambda last: pass_moved(k, h, last).wait_send())
            pl.when(has_north)(lambda: south_m_copy.wait_send())
            west_copy.wait_send()
            back_west.wait_send()
            pl.when(has_south)(lambda: back_south.wait_send())
            back_east.wait_send()
            back_north.wait_send()

    for d in (1, 2, 3):
        scaled_copy(sa, peers[d]).wait_send()
        part_copy(sa, peers[d]).wait_send()


def on_device(nx, ny, source, group_gain, shot_group, block_cols, block_vals):
    vmem, smem, hbm = (pl.BlockSpec(memory_space=m) for m in (pltpu.VMEM, pltpu.SMEM, pl.ANY))
    dma = pltpu.SemaphoreType.DMA
    bf16, f32 = jnp.bfloat16, jnp.float32
    trace = pltpu.VMEM((NT * N, BLK), bf16)
    cols = block_cols[0, 0].T
    outs = pl.pallas_call(
        functools.partial(kernel, nx, ny),
        out_shape=[jax.ShapeDtypeStruct((N, NT * BLK), bf16), jax.ShapeDtypeStruct((N, NT * BLK), bf16),
                   jax.ShapeDtypeStruct((N, (OUTB - TRACED) * BLK), bf16)],
        in_specs=[vmem, smem, smem, smem, hbm, hbm],
        out_specs=[vmem, vmem, vmem],
        scratch_shapes=[
            pltpu.VMEM((OUTB, 2, BLK, BLK), bf16),
            pltpu.VMEM((OWN, 4, BLK, BLK), bf16),
            pltpu.VMEM((SA, NS * N, BLK), bf16),
            pltpu.VMEM((NS, SA * N, BLK), f32),
            pltpu.VMEM((SA, OWN, N, BLK), f32),
            pltpu.VMEM((SA, OWN, N, BLK), f32),
            pltpu.VMEM((NS + 2 * NT, N, BLK), f32),
            trace, trace, trace, trace,
            *[pltpu.VMEM((SA, sent, BLK, BLK), bf16) for sent in SENT],
            *[pltpu.VMEM(((SA - 1) * lot, BLK, BLK), bf16) for lot in LOT],
            pltpu.VMEM((TRACED * N, BLK), bf16),
            pltpu.VMEM((TRACED * N, BLK), bf16),
            pltpu.VMEM(cols.shape, jnp.int32),
            pltpu.SMEM(cols.shape, jnp.int32),
            pltpu.VMEM((NS + 2 * NT, N, BLK), f32),
            trace, trace, trace,
            dma, dma((2, SA)), dma((2, SA)), dma((SA,)), dma((SA,)), dma((SA,)), dma((SA,)), dma((7,)), dma((5,)),
            dma((2,)), dma((2, SA - 1)), dma((2, 2)), dma((2,)), dma((2,)), dma((2, 2, SA)), dma((2, 2, SA)), dma((2,)), dma((2, 2)),
            pltpu.SemaphoreType.REGULAR, pltpu.SemaphoreType.REGULAR,
        ],
        compiler_params=pltpu.CompilerParams(collective_id=0, has_side_effects=True, vmem_limit_bytes=63 << 20),
        name="sweep",
    )(source[0, 0], group_gain, shot_group, cols, cols, block_vals[0, 0])
    return tuple(out[None, None] for out in outs)


def solution(mesh):
    placed = (
        P("gx", "gy", "sa", None),
        P(),
        P("sa"),
        P("gx", "gy", None, None),
        P("gx", "gy", "sa", None, None, None),
    )
    return jax.shard_map(
        functools.partial(on_device, mesh.shape["gx"], mesh.shape["gy"]),
        mesh=mesh,
        in_specs=placed,
        out_specs=(P("gx", "gy", "sa", None), P("gx", "gy", "sa", None), P("gx", "gy", "sa", None)),
        check_vma=False,
    )
```

```python
import functools

import jax
import jax.numpy as jnp
from jax import lax
from jax.experimental import pallas as pl
from jax.experimental.pallas import tpu as pltpu
from jax.sharding import PartitionSpec as P

MESH = pl.DeviceIdType.MESH
BLK = 128
NT = 12
NS = 6
OUTB = 32
SA = 4
OWN = OUTB // SA
N = 8
TRACED = 2 * NT
CHUNKS = ((0, 0), (0, 1), (1, 0), (1, 1))
SENT = (6, 7)
LOT = tuple(OWN - sent for sent in SENT)


STEP = 2


def piece(k, h, last):
    count = (SA - 1) * LOT[k] if last else SENT[k]
    first = (count + 1) // 2
    return pl.ds(first, count - first) if h else pl.ds(0, first)


def sent_slot(o, k):
    owner, r = divmod(o, OWN)
    return (owner, r) if r < SENT[k] else (SA - 1, LOT[k] * owner + r - SENT[k])


def each(owner, act):
    pl.when(owner < SA - 1)(lambda: act(False))
    pl.when(owner == SA - 1)(lambda: act(True))


def kernel(nx, ny, source, gain, group, cols, cols_hbm, vals_hbm, east_out, north_out, inner_out,
           weights, vals, scaled_all, picked_src, part_send, part, traces, west, south, east, north,
           moved_w, moved_s, stage_w, stage_s, part_moved, part_m, cols_vmem, cols_m, traces_m, south_m, east_m, north_m,
           local_sem, w_send, w_recv, s_send, s_recv, p_send, p_recv, t_send, t_recv,
           h_send, h_recv, z_send, z_more, e_recv, m_send, m_recv, f_send, f_moved, go_sem, ack_sem):
    gx, gy, sa = lax.axis_index("gx"), lax.axis_index("gy"), lax.axis_index("sa")
    moved, stage = (moved_w, moved_s), (stage_w, stage_s)
    odd = lax.rem(gx, 2)
    z = gy // 2
    peers = [lax.rem(sa + d, SA) for d in range(SA)]
    donor = (odd == 1) & (gx < nx - 1)
    host = (odd == 0) & (gx < nx - 2)
    works = jnp.logical_not(donor)
    ends = gx == nx - 1
    before_end = gx == nx - 2
    has_west, has_south, has_north = gx > 0, gy > 0, gy < ny - 1
    z_odd = lax.rem(z, 2) == 1
    chained = donor & z_odd
    chains = chained & (gy < ny - 4)

    barrier = pltpu.get_barrier_semaphore()
    near = (
        ((odd == 0) & (gx < nx - 2), 2, 0), ((odd == 0) & (gx > 1), -2, 0),
        (works & has_south, 0, -1), (works & has_north, 0, 1),
        (chained & (gy >= 4), 0, -4), (chains, 0, 4),
    )
    for there, dx, dy in ((odd == 0, 1, 0),) + near:
        @pl.when(there)
        def _():
            pl.semaphore_signal(barrier, inc=1, device_id=(gx + dx, gy + dy, sa), device_id_type=MESH)
    for d in range(1, SA):
        pl.semaphore_signal(barrier, inc=1, device_id=(gx, gy, peers[d]), device_id_type=MESH)

    load = pltpu.make_async_copy(vals_hbm, vals, local_sem)
    load.start()

    shot = lax.broadcasted_iota(jnp.int32, (N, BLK), 0)
    gains = jnp.zeros((N, BLK), jnp.float32)
    for s in range(N):
        gains = jnp.where(shot == s, gain[group[s]], gains)
    for pair in range(NS // 2):
        halves = [source[:, (2 * pair + h) * BLK:(2 * pair + h + 1) * BLK].astype(jnp.float32) * gains for h in (0, 1)]
        scaled_all[sa, pair * 16:(pair + 1) * 16, :] = jnp.concatenate(halves, axis=0).astype(jnp.bfloat16)

    load.wait()
    pl.semaphore_wait(barrier, 3 + odd + sum(there.astype(jnp.int32) for there, _, _ in near))

    def copy(src, dst, send, recv, dx=0, dy=0, to=None):
        return pltpu.make_async_remote_copy(src, dst, send, recv, device_id=(gx + dx, gy + dy, sa if to is None else to),
                                            device_id_type=MESH)

    def scaled_copy(owner, peer):
        return copy(scaled_all.at[owner], scaled_all.at[owner], s_send.at[peer], s_recv.at[owner], to=peer)

    def part_copy(owner, peer):
        return copy(part_send.at[peer], part.at[owner], p_send.at[peer], p_recv.at[owner], to=peer)

    def weight_copy(k, owner, peer):
        rows = pl.ds(owner * OWN, OWN)
        return copy(vals.at[:, k:k + 1], weights.at[rows, k:k + 1], w_send.at[k, peer], w_recv.at[k, owner], to=peer)

    def own_copy(k, p):
        rows = pl.ds(p * OWN, OWN)
        return pltpu.make_async_copy(vals.at[:, k:k + 1], weights.at[rows, k:k + 1], w_recv.at[k, p])

    needed = (has_west, has_south)

    def weights_do(act, ds):
        for k in (1, 0):
            @pl.when(needed[k])
            def _():
                for d in ds:
                    act(weight_copy(k, sa, peers[d]))

    def send_interior():
        weights_do(lambda c: c.start(), (2, 1, 3))

    def arrived(p):
        for k in (1, 0):
            @pl.when(needed[k])
            def _():
                own_copy(k, p).wait()

    def pass_on(k, d):
        rows = pl.ds(peers[d] * OWN, OWN)
        ref = weights.at[rows, k:k + 1]
        return copy(ref, ref, f_send.at[k], w_recv.at[k, peers[d]], to=peers[SA - d])

    def pass_moved(k, h, last):
        d = 1 if h else SA - 1
        ref = moved[k].at[peers[d], piece(k, h, last)]
        return copy(ref, ref, f_moved.at[k, h], m_recv.at[k, h, peers[d]], to=peers[SA - d])

    def shuffle_copy(k, owner):
        return copy(vals.at[pl.ds(SENT[k], LOT[k]), k], stage[k].at[pl.ds(owner * LOT[k], LOT[k])], h_send.at[k],
                    h_recv.at[k, owner], to=SA - 1)

    def move_copy(k, h, last):
        rows = piece(k, h, last)
        src = stage[k].at[rows] if last else vals.at[rows, k]
        return copy(src, moved[k].at[sa, rows], z_send.at[k, h], m_recv.at[k, h, sa], dx=-1)

    def moved_copy(k, h, owner, peer, last):
        ref = moved[k].at[owner, piece(k, h, last)]
        return copy(ref, ref, m_send.at[k, h, peer], m_recv.at[k, h, owner], to=peer)

    part_move = copy(part_moved, part_m, z_more.at[0], e_recv.at[0], dx=-1)
    cols_move = copy(cols_hbm, cols_vmem, z_more.at[1], e_recv.at[1], dx=-1)

    def moves(act, chunks):
        for last in (False, True):
            @pl.when((sa == SA - 1) if last else (sa < SA - 1))
            def _():
                for k, h in chunks:
                    pl.when(needed[k])(lambda: act(move_copy(k, h, last)))

    gated = jnp.logical_not(z_odd) & (z >= 4)

    def start_moves():
        pl.when(jnp.logical_not(gated))(lambda: moves(lambda c: c.start(), CHUNKS))

        @pl.when(gated)
        def _():
            for k, h in CHUNKS:
                def bit_by_bit(last):
                    src = stage[k] if last else vals.at[:, k]
                    rows = piece(k, h, last)
                    for r in range(rows.start, rows.start + rows.size, STEP):
                        some = pl.ds(r, min(STEP, rows.start + rows.size - r))
                        c = copy(src.at[some], moved[k].at[sa, some], z_send.at[k, h], m_recv.at[k, h, sa], dx=-1)
                        c.start()
                        c.wait_send()
                pl.when(needed[k])(lambda: each(sa, bit_by_bit))

    early = donor & (jnp.logical_not(z_odd) | (z == 1))
    late = donor & z_odd & (z > 1)

    @pl.when(donor & (sa < SA - 1))
    def _():
        for k in (0, 1):
            shuffle_copy(k, sa).start()
    pl.when(donor)(lambda: cols_move.start())
    pl.when(early & (sa < SA - 1))(start_moves)
    for d in (2, 1, 3):
        scaled_copy(sa, peers[d]).start()
    pl.when(ends)(lambda: pl.semaphore_signal(ack_sem, inc=1, device_id=(gx - 1, gy, sa), device_id_type=MESH))

    @pl.when(donor & (sa == SA - 1))
    def _():
        for owner in range(SA - 1):
            for k in (0, 1):
                shuffle_copy(k, owner).wait_recv()
        pl.when(early)(start_moves)

    for d in (1, 3, 2):
        scaled_copy(peers[d], peers[d]).wait_recv()
    for p in range(SA):
        for pair in range(NS // 2):
            both = scaled_all[p, pair * 16:(pair + 1) * 16, :].astype(jnp.float32)
            picked_src[2 * pair, p * N:(p + 1) * N, :] = both[:N]
            picked_src[2 * pair + 1, p * N:(p + 1) * N, :] = both[N:]
    for r in range(OWN):
        o = sa * OWN + r
        left = jnp.concatenate([picked_src[cols[2, o]], picked_src[cols[3, o]]], axis=1).astype(jnp.bfloat16)
        out = jnp.dot(left, vals[r, 2:4].reshape(2 * BLK, BLK), preferred_element_type=jnp.float32)
        for p in range(SA):
            part_send[p, r] = out[p * N:(p + 1) * N]
    for d in (2, 1, 3):
        part_copy(sa, peers[d]).start()

    pl.when(works & (sa < SA - 1))(lambda: weights_do(lambda c: c.start(), (1, 3)))
    gathers = works | (sa == SA - 1)
    for k in (1, 0):
        @pl.when(needed[k] & gathers)
        def _():
            own_copy(k, sa).start()

        @pl.when(jnp.logical_not(needed[k]))
        def _():
            weights[:, k] = jnp.zeros((OUTB, BLK, BLK), jnp.bfloat16)
    part[sa] = part_send[sa]
    for d in (1, 3, 2):
        part_copy(peers[d], peers[d]).wait_recv()

    def unpack(ref, dst, base):
        for pair in range(NT // 2):
            both = ref[pair * 16:(pair + 1) * 16, :].astype(jnp.float32)
            dst[base + 2 * pair] = both[:N]
            dst[base + 2 * pair + 1] = both[N:]

    def clear(dst, base):
        for b in range(NT):
            dst[base + b] = jnp.zeros((N, BLK), jnp.float32)

    def row(o):
        left = jnp.concatenate([traces[cols[0, o]], traces[cols[1, o]]], axis=1).astype(jnp.bfloat16)
        out = jnp.dot(left, weights[o].reshape(2 * BLK, BLK), preferred_element_type=jnp.float32)
        return out + part[o // OWN, o % OWN]

    def row_m(o):
        left = jnp.concatenate([traces_m[cols_m[0, o]], traces_m[cols_m[1, o]]], axis=1).astype(jnp.bfloat16)
        blocks = jnp.concatenate([moved[k][sent_slot(o, k)] for k in (0, 1)], axis=0)
        return jnp.dot(left, blocks, preferred_element_type=jnp.float32)

    def interior():
        for o in range(TRACED, OUTB):
            inner_out[:, (o - TRACED) * BLK:(o - TRACED + 1) * BLK] = row(o).astype(jnp.bfloat16)

    def put_out():
        for ref, out in ((east, east_out), (north, north_out)):
            for pair in range(NT // 2):
                both = ref[pair * 16:(pair + 1) * 16, :]
                out[:, 2 * pair * BLK:(2 * pair + 1) * BLK] = both[:N]
                out[:, (2 * pair + 1) * BLK:(2 * pair + 2) * BLK] = both[N:]

    west_copy = copy(east_m, west, t_send.at[0], t_recv.at[0], dx=2)
    west_end_copy = copy(east, west, t_send.at[0], t_recv.at[0], dx=1)
    south_copy = copy(north, south, t_send.at[1], t_recv.at[1], dy=1)
    south_m_copy = copy(north_m, south_m, t_send.at[2], t_recv.at[2], dy=1)
    back_west = copy(east, west, t_send.at[3], t_recv.at[0], dx=1)
    back_south = copy(south_m, south, t_send.at[4], t_recv.at[1], dx=1)
    back_east = copy(east_m, east, t_send.at[5], t_recv.at[3], dx=1)
    back_north = copy(north_m, north, t_send.at[6], t_recv.at[4], dx=1)

    @pl.when(donor)
    def _():
        for o in range(0, TRACED, 2):
            both = jnp.concatenate([part[o // OWN, o % OWN], part[o // OWN, o % OWN + 1]], axis=0)
            part_moved[o * N:(o + 2) * N, :] = both.astype(jnp.bfloat16)

        @pl.when(late)
        def _():
            pl.semaphore_wait(go_sem, 1)
            start_moves()
        part_move.start()
        pl.when(jnp.logical_not(gated))(lambda: moves(lambda c: c.wait_send(), CHUNKS))
        part_move.wait_send()

        @pl.when(chains)
        def _():
            pl.semaphore_signal(go_sem, inc=1, device_id=(gx, gy + 4, sa), device_id_type=MESH)
        pl.when(sa == SA - 1)(send_interior)
        arrived(SA - 1)
        back_west.wait_recv()
        unpack(west, traces, NS)

        @pl.when(has_south)
        def _():
            back_south.wait_recv()
            unpack(south, traces, NS + NT)
        pl.when(jnp.logical_not(has_south))(lambda: clear(traces, NS + NT))
        interior()
        back_east.wait_recv()
        back_north.wait_recv()
        put_out()
        cols_move.wait_send()
        for k in (0, 1):
            pl.when(sa < SA - 1)(lambda: shuffle_copy(k, sa).wait_send())

        pl.when(sa == SA - 1)(lambda: weights_do(lambda c: c.wait_send(), (1, 2, 3)))

    passes = ((1, 1), (0, 3))

    @pl.when(works)
    def _():
        for k, d in passes:
            @pl.when(needed[k] & (peers[d] < SA - 1))
            def _():
                own_copy(k, peers[d]).wait()
                pass_on(k, d).start()
        for d in range(SA):
            for k in (1, 0):
                if (k, d) not in passes:
                    @pl.when(needed[k] & (peers[d] < SA - 1))
                    def _():
                        own_copy(k, peers[d]).wait()
        pl.when((sa == SA - 1) & ((gx >= nx - 2) | (z >= 4)))(send_interior)

    needed_m = (gx >= 0, has_south)

    def do_native():
        @pl.when(has_south)
        def _():
            south_copy.wait_recv()
            unpack(south, traces, NS + NT)
        pl.when(jnp.logical_not(has_south))(lambda: clear(traces, NS + NT))
        @pl.when(has_west)
        def _():
            west_copy.wait_recv()
            unpack(west, traces, NS)
        pl.when(jnp.logical_not(has_west))(lambda: clear(traces, NS))
        for base, ref in ((NT, north), (0, east)):
            for o in range(base, base + NT, 2):
                both = jnp.concatenate([row(o), row(o + 1)], axis=0)
                ref[(o - base) * N:(o - base + 2) * N, :] = both.astype(jnp.bfloat16)
            if base:
                pl.when(has_north)(lambda: south_copy.start())

        @pl.when(before_end)
        def _():
            pl.semaphore_wait(ack_sem, 1)
            west_end_copy.start()

    @pl.when(host)
    def _():
        @pl.when(jnp.logical_not(has_south))
        def _():
            for p in range(SA):
                moved[1][p] = jnp.zeros((SENT[1], BLK, BLK), jnp.bfloat16)
        for k, h in CHUNKS:
            @pl.when(needed_m[k])
            def _():
                def move_on(last):
                    moved_copy(k, h, sa, peers[1], last).wait_recv()
                    for d in (1, 3):
                        moved_copy(k, h, sa, peers[d], last).start()
                each(sa, move_on)
        for k, h in CHUNKS:
            @pl.when(needed_m[k])
            def _():
                def move_on(last):
                    moved_copy(k, h, peers[1 if h else SA - 1], sa, last).wait_recv()
                    pass_moved(k, h, last).start()
                each(peers[1 if h else SA - 1], move_on)
        cols_move.wait_recv()
        to_smem = pltpu.make_async_copy(cols_vmem, cols_m, local_sem)
        to_smem.start()
        to_smem.wait()
        part_move.wait_recv()
        for k, h in CHUNKS:
            @pl.when(needed_m[k])
            def _():
                for d in (SA - 1 if h else 1, 2):
                    each(peers[d], lambda last: moved_copy(k, h, peers[d], sa, last).wait_recv())

    pl.when(works)(do_native)

    @pl.when(host)
    def _():
        unpack(east, traces_m, NS)

        @pl.when(has_south)
        def _():
            south_m_copy.wait_recv()
            unpack(south_m, traces_m, NS + NT)
        pl.when(jnp.logical_not(has_south))(lambda: clear(traces_m, NS + NT))
        for base, ref in ((NT, north_m), (0, east_m)):
            for o in range(base, base + NT, 2):
                both = jnp.concatenate([row_m(o), row_m(o + 1)], axis=0)
                both = (both + part_m[o * N:(o + 2) * N, :].astype(jnp.float32)).astype(jnp.bfloat16)
                ref[(o - base) * N:(o - base + 2) * N, :] = both
            if base:
                pl.when(has_north)(lambda: south_m_copy.start())
        west_copy.start()
        back_west.start()
        pl.when(has_south)(lambda: back_south.start())
        back_east.start()
        back_north.start()
        pl.when((sa == SA - 1) & (z < 4))(send_interior)

    @pl.when(works)
    def _():
        arrived(SA - 1)
        interior()
        put_out()
        pl.when(sa < SA - 1)(lambda: weights_do(lambda c: c.wait_send(), (1, 3)))
        pl.when(sa == SA - 1)(lambda: weights_do(lambda c: c.wait_send(), (1, 2, 3)))
        for k, d in passes:
            pl.when(needed[k] & (peers[d] < SA - 1))(lambda: pass_on(k, d).wait_send())
        pl.when(has_north)(lambda: south_copy.wait_send())
        pl.when(before_end)(lambda: west_end_copy.wait_send())

        @pl.when(host)
        def _():
            for k, h in CHUNKS:
                @pl.when(needed_m[k])
                def _():
                    for d in (1, 3):
                        each(sa, lambda last: moved_copy(k, h, sa, peers[d], last).wait_send())
                    each(peers[1 if h else SA - 1], lambda last: pass_moved(k, h, last).wait_send())
            pl.when(has_north)(lambda: south_m_copy.wait_send())
            west_copy.wait_send()
            back_west.wait_send()
            pl.when(has_south)(lambda: back_south.wait_send())
            back_east.wait_send()
            back_north.wait_send()

    for d in (1, 2, 3):
        scaled_copy(sa, peers[d]).wait_send()
        part_copy(sa, peers[d]).wait_send()


def on_device(nx, ny, source, group_gain, shot_group, block_cols, block_vals):
    vmem, smem, hbm = (pl.BlockSpec(memory_space=m) for m in (pltpu.VMEM, pltpu.SMEM, pl.ANY))
    dma = pltpu.SemaphoreType.DMA
    bf16, f32 = jnp.bfloat16, jnp.float32
    trace = pltpu.VMEM((NT * N, BLK), bf16)
    cols = block_cols[0, 0].T
    outs = pl.pallas_call(
        functools.partial(kernel, nx, ny),
        out_shape=[jax.ShapeDtypeStruct((N, NT * BLK), bf16), jax.ShapeDtypeStruct((N, NT * BLK), bf16),
                   jax.ShapeDtypeStruct((N, (OUTB - TRACED) * BLK), bf16)],
        in_specs=[vmem, smem, smem, smem, hbm, hbm],
        out_specs=[vmem, vmem, vmem],
        scratch_shapes=[
            pltpu.VMEM((OUTB, 2, BLK, BLK), bf16),
            pltpu.VMEM((OWN, 4, BLK, BLK), bf16),
            pltpu.VMEM((SA, NS * N, BLK), bf16),
            pltpu.VMEM((NS, SA * N, BLK), f32),
            pltpu.VMEM((SA, OWN, N, BLK), f32),
            pltpu.VMEM((SA, OWN, N, BLK), f32),
            pltpu.VMEM((NS + 2 * NT, N, BLK), f32),
            trace, trace, trace, trace,
            *[pltpu.VMEM((SA, sent, BLK, BLK), bf16) for sent in SENT],
            *[pltpu.VMEM(((SA - 1) * lot, BLK, BLK), bf16) for lot in LOT],
            pltpu.VMEM((TRACED * N, BLK), bf16),
            pltpu.VMEM((TRACED * N, BLK), bf16),
            pltpu.VMEM(cols.shape, jnp.int32),
            pltpu.SMEM(cols.shape, jnp.int32),
            pltpu.VMEM((NS + 2 * NT, N, BLK), f32),
            trace, trace, trace,
            dma, dma((2, SA)), dma((2, SA)), dma((SA,)), dma((SA,)), dma((SA,)), dma((SA,)), dma((7,)), dma((5,)),
            dma((2,)), dma((2, SA - 1)), dma((2, 2)), dma((2,)), dma((2,)), dma((2, 2, SA)), dma((2, 2, SA)), dma((2,)), dma((2, 2)),
            pltpu.SemaphoreType.REGULAR, pltpu.SemaphoreType.REGULAR,
        ],
        compiler_params=pltpu.CompilerParams(collective_id=0, has_side_effects=True, vmem_limit_bytes=107 << 19),
        name="sweep",
    )(source[0, 0], group_gain, shot_group, cols, cols, block_vals[0, 0])
    return tuple(out[None, None] for out in outs)


def solution(mesh):
    placed = (
        P("gx", "gy", "sa", None),
        P(),
        P("sa"),
        P("gx", "gy", None, None),
        P("gx", "gy", "sa", None, None, None),
    )
    return jax.shard_map(
        functools.partial(on_device, mesh.shape["gx"], mesh.shape["gy"]),
        mesh=mesh,
        in_specs=placed,
        out_specs=(P("gx", "gy", "sa", None), P("gx", "gy", "sa", None), P("gx", "gy", "sa", None)),
        check_vma=False,
    )
```

```python
import functools

import jax
import jax.numpy as jnp
from jax import lax
from jax.experimental import pallas as pl
from jax.experimental.pallas import tpu as pltpu
from jax.sharding import PartitionSpec as P

MESH = pl.DeviceIdType.MESH
BLK = 128
NT = 12
NS = 6
OUTB = 32
SA = 4
OWN = OUTB // SA
N = 8
TRACED = 2 * NT
CHUNKS = ((0, 0), (0, 1), (1, 0), (1, 1))
SENT = (6, 7)
LOT = tuple(OWN - sent for sent in SENT)


STEP = 2


def piece(k, h, last):
    count = (SA - 1) * LOT[k] if last else SENT[k]
    first = (count + 1) // 2
    return pl.ds(first, count - first) if h else pl.ds(0, first)


def sent_slot(o, k):
    owner, r = divmod(o, OWN)
    return (owner, r) if r < SENT[k] else (SA - 1, LOT[k] * owner + r - SENT[k])


def each(owner, act):
    pl.when(owner < SA - 1)(lambda: act(False))
    pl.when(owner == SA - 1)(lambda: act(True))


def kernel(nx, ny, source, gain, group, cols, cols_hbm, vals_hbm, east_out, north_out, inner_out,
           weights, vals, scaled_all, picked_src, part_send, part, traces, west, south, east, north,
           moved_w, moved_s, stage_w, stage_s, part_moved, part_m, cols_vmem, cols_m, traces_m, south_m, east_m, north_m,
           local_sem, w_send, w_recv, s_send, s_recv, p_send, p_recv, t_send, t_recv,
           h_send, h_recv, z_send, z_more, e_recv, m_send, m_recv, f_send, f_moved, go_sem, ack_sem):
    gx, gy, sa = lax.axis_index("gx"), lax.axis_index("gy"), lax.axis_index("sa")
    moved, stage = (moved_w, moved_s), (stage_w, stage_s)
    odd = lax.rem(gx, 2)
    z = gy // 2
    peers = [lax.rem(sa + d, SA) for d in range(SA)]
    donor = (odd == 1) & (gx < nx - 1)
    host = (odd == 0) & (gx < nx - 2)
    works = jnp.logical_not(donor)
    ends = gx == nx - 1
    before_end = gx == nx - 2
    has_west, has_south, has_north = gx > 0, gy > 0, gy < ny - 1
    z_odd = lax.rem(z, 2) == 1
    chained = donor & z_odd
    chains = chained & (gy < ny - 4)

    barrier = pltpu.get_barrier_semaphore()
    near = (
        ((odd == 0) & (gx < nx - 2), 2, 0), ((odd == 0) & (gx > 1), -2, 0),
        (works & has_south, 0, -1), (works & has_north, 0, 1),
        (chained & (gy >= 4), 0, -4), (chains, 0, 4),
    )
    for there, dx, dy in ((odd == 0, 1, 0),) + near:
        @pl.when(there)
        def _():
            pl.semaphore_signal(barrier, inc=1, device_id=(gx + dx, gy + dy, sa), device_id_type=MESH)
    for d in range(1, SA):
        pl.semaphore_signal(barrier, inc=1, device_id=(gx, gy, peers[d]), device_id_type=MESH)

    load = pltpu.make_async_copy(vals_hbm, vals, local_sem)
    load.start()

    shot = lax.broadcasted_iota(jnp.int32, (N, BLK), 0)
    gains = jnp.zeros((N, BLK), jnp.float32)
    for s in range(N):
        gains = jnp.where(shot == s, gain[group[s]], gains)
    for pair in range(NS // 2):
        halves = [source[:, (2 * pair + h) * BLK:(2 * pair + h + 1) * BLK].astype(jnp.float32) * gains for h in (0, 1)]
        scaled_all[sa, pair * 16:(pair + 1) * 16, :] = jnp.concatenate(halves, axis=0).astype(jnp.bfloat16)

    load.wait()
    pl.semaphore_wait(barrier, 3 + odd + sum(there.astype(jnp.int32) for there, _, _ in near))

    def copy(src, dst, send, recv, dx=0, dy=0, to=None):
        return pltpu.make_async_remote_copy(src, dst, send, recv, device_id=(gx + dx, gy + dy, sa if to is None else to),
                                            device_id_type=MESH)

    def scaled_copy(owner, peer):
        return copy(scaled_all.at[owner], scaled_all.at[owner], s_send.at[peer], s_recv.at[owner], to=peer)

    def part_copy(owner, peer):
        return copy(part_send.at[peer], part.at[owner], p_send.at[peer], p_recv.at[owner], to=peer)

    def weight_copy(k, owner, peer):
        rows = pl.ds(owner * OWN, OWN)
        return copy(vals.at[:, k:k + 1], weights.at[rows, k:k + 1], w_send.at[k, peer], w_recv.at[k, owner], to=peer)

    def own_copy(k, p):
        rows = pl.ds(p * OWN, OWN)
        return pltpu.make_async_copy(vals.at[:, k:k + 1], weights.at[rows, k:k + 1], w_recv.at[k, p])

    needed = (has_west, has_south)

    def weights_do(act, ds):
        for k in (1, 0):
            @pl.when(needed[k])
            def _():
                for d in ds:
                    act(weight_copy(k, sa, peers[d]))

    def send_interior():
        weights_do(lambda c: c.start(), (2, 1, 3))

    def arrived(p):
        for k in (1, 0):
            @pl.when(needed[k])
            def _():
                own_copy(k, p).wait()

    def pass_on(k, d):
        rows = pl.ds(peers[d] * OWN, OWN)
        ref = weights.at[rows, k:k + 1]
        return copy(ref, ref, f_send.at[k], w_recv.at[k, peers[d]], to=peers[SA - d])

    def pass_moved(k, h, last):
        d = 1 if h else SA - 1
        ref = moved[k].at[peers[d], piece(k, h, last)]
        return copy(ref, ref, f_moved.at[k, h], m_recv.at[k, h, peers[d]], to=peers[SA - d])

    def shuffle_copy(k, owner):
        return copy(vals.at[pl.ds(SENT[k], LOT[k]), k], stage[k].at[pl.ds(owner * LOT[k], LOT[k])], h_send.at[k],
                    h_recv.at[k, owner], to=SA - 1)

    def move_copy(k, h, last):
        rows = piece(k, h, last)
        src = stage[k].at[rows] if last else vals.at[rows, k]
        return copy(src, moved[k].at[sa, rows], z_send.at[k, h], m_recv.at[k, h, sa], dx=-1)

    def moved_copy(k, h, owner, peer, last):
        ref = moved[k].at[owner, piece(k, h, last)]
        return copy(ref, ref, m_send.at[k, h, peer], m_recv.at[k, h, owner], to=peer)

    part_move = copy(part_moved, part_m, z_more.at[0], e_recv.at[0], dx=-1)
    cols_move = copy(cols_hbm, cols_vmem, z_more.at[1], e_recv.at[1], dx=-1)

    def moves(act, chunks):
        for last in (False, True):
            @pl.when((sa == SA - 1) if last else (sa < SA - 1))
            def _():
                for k, h in chunks:
                    pl.when(needed[k])(lambda: act(move_copy(k, h, last)))

    gated = jnp.logical_not(z_odd) & (z >= 2)

    def start_moves():
        pl.when(jnp.logical_not(gated))(lambda: moves(lambda c: c.start(), CHUNKS))

        @pl.when(gated)
        def _():
            for k, h in CHUNKS:
                def bit_by_bit(last):
                    src = stage[k] if last else vals.at[:, k]
                    rows = piece(k, h, last)
                    for r in range(rows.start, rows.start + rows.size, STEP):
                        some = pl.ds(r, min(STEP, rows.start + rows.size - r))
                        c = copy(src.at[some], moved[k].at[sa, some], z_send.at[k, h], m_recv.at[k, h, sa], dx=-1)
                        c.start()
                        c.wait_send()
                pl.when(needed[k])(lambda: each(sa, bit_by_bit))

    early = donor & (jnp.logical_not(z_odd) | (z == 1))
    late = donor & z_odd & (z > 1)

    @pl.when(donor & (sa < SA - 1))
    def _():
        for k in (0, 1):
            shuffle_copy(k, sa).start()
    pl.when(donor)(lambda: cols_move.start())
    pl.when(early & (sa < SA - 1))(start_moves)
    for d in (2, 1, 3):
        scaled_copy(sa, peers[d]).start()
    pl.when(ends)(lambda: pl.semaphore_signal(ack_sem, inc=1, device_id=(gx - 1, gy, sa), device_id_type=MESH))

    @pl.when(donor & (sa == SA - 1))
    def _():
        for owner in range(SA - 1):
            for k in (0, 1):
                shuffle_copy(k, owner).wait_recv()
        pl.when(early)(start_moves)

    for d in (1, 3, 2):
        scaled_copy(peers[d], peers[d]).wait_recv()
    for p in range(SA):
        for pair in range(NS // 2):
            both = scaled_all[p, pair * 16:(pair + 1) * 16, :].astype(jnp.float32)
            picked_src[2 * pair, p * N:(p + 1) * N, :] = both[:N]
            picked_src[2 * pair + 1, p * N:(p + 1) * N, :] = both[N:]
    for r in range(OWN):
        o = sa * OWN + r
        left = jnp.concatenate([picked_src[cols[2, o]], picked_src[cols[3, o]]], axis=1).astype(jnp.bfloat16)
        out = jnp.dot(left, vals[r, 2:4].reshape(2 * BLK, BLK), preferred_element_type=jnp.float32)
        for p in range(SA):
            part_send[p, r] = out[p * N:(p + 1) * N]
    for d in (2, 1, 3):
        part_copy(sa, peers[d]).start()

    pl.when(works & (sa < SA - 1))(lambda: weights_do(lambda c: c.start(), (1, 3)))
    gathers = works | (sa == SA - 1)
    for k in (1, 0):
        @pl.when(needed[k] & gathers)
        def _():
            own_copy(k, sa).start()

        @pl.when(jnp.logical_not(needed[k]))
        def _():
            weights[:, k] = jnp.zeros((OUTB, BLK, BLK), jnp.bfloat16)
    part[sa] = part_send[sa]
    for d in (1, 3, 2):
        part_copy(peers[d], peers[d]).wait_recv()

    def unpack(ref, dst, base):
        for pair in range(NT // 2):
            both = ref[pair * 16:(pair + 1) * 16, :].astype(jnp.float32)
            dst[base + 2 * pair] = both[:N]
            dst[base + 2 * pair + 1] = both[N:]

    def clear(dst, base):
        for b in range(NT):
            dst[base + b] = jnp.zeros((N, BLK), jnp.float32)

    def row(o):
        left = jnp.concatenate([traces[cols[0, o]], traces[cols[1, o]]], axis=1).astype(jnp.bfloat16)
        out = jnp.dot(left, weights[o].reshape(2 * BLK, BLK), preferred_element_type=jnp.float32)
        return out + part[o // OWN, o % OWN]

    def row_m(o):
        left = jnp.concatenate([traces_m[cols_m[0, o]], traces_m[cols_m[1, o]]], axis=1).astype(jnp.bfloat16)
        blocks = jnp.concatenate([moved[k][sent_slot(o, k)] for k in (0, 1)], axis=0)
        return jnp.dot(left, blocks, preferred_element_type=jnp.float32)

    def interior():
        for o in range(TRACED, OUTB):
            inner_out[:, (o - TRACED) * BLK:(o - TRACED + 1) * BLK] = row(o).astype(jnp.bfloat16)

    def put_out():
        for ref, out in ((east, east_out), (north, north_out)):
            for pair in range(NT // 2):
                both = ref[pair * 16:(pair + 1) * 16, :]
                out[:, 2 * pair * BLK:(2 * pair + 1) * BLK] = both[:N]
                out[:, (2 * pair + 1) * BLK:(2 * pair + 2) * BLK] = both[N:]

    west_copy = copy(east_m, west, t_send.at[0], t_recv.at[0], dx=2)
    west_end_copy = copy(east, west, t_send.at[0], t_recv.at[0], dx=1)
    south_copy = copy(north, south, t_send.at[1], t_recv.at[1], dy=1)
    south_m_copy = copy(north_m, south_m, t_send.at[2], t_recv.at[2], dy=1)
    back_west = copy(east, west, t_send.at[3], t_recv.at[0], dx=1)
    back_south = copy(south_m, south, t_send.at[4], t_recv.at[1], dx=1)
    back_east = copy(east_m, east, t_send.at[5], t_recv.at[3], dx=1)
    back_north = copy(north_m, north, t_send.at[6], t_recv.at[4], dx=1)

    @pl.when(donor)
    def _():
        for o in range(0, TRACED, 2):
            both = jnp.concatenate([part[o // OWN, o % OWN], part[o // OWN, o % OWN + 1]], axis=0)
            part_moved[o * N:(o + 2) * N, :] = both.astype(jnp.bfloat16)

        @pl.when(late)
        def _():
            pl.semaphore_wait(go_sem, 1)
            start_moves()
        part_move.start()
        pl.when(jnp.logical_not(gated))(lambda: moves(lambda c: c.wait_send(), CHUNKS))
        part_move.wait_send()

        @pl.when(chains)
        def _():
            pl.semaphore_signal(go_sem, inc=1, device_id=(gx, gy + 4, sa), device_id_type=MESH)
        pl.when(sa == SA - 1)(send_interior)
        arrived(SA - 1)
        back_west.wait_recv()
        unpack(west, traces, NS)

        @pl.when(has_south)
        def _():
            back_south.wait_recv()
            unpack(south, traces, NS + NT)
        pl.when(jnp.logical_not(has_south))(lambda: clear(traces, NS + NT))
        interior()
        back_east.wait_recv()
        back_north.wait_recv()
        put_out()
        cols_move.wait_send()
        for k in (0, 1):
            pl.when(sa < SA - 1)(lambda: shuffle_copy(k, sa).wait_send())

        pl.when(sa == SA - 1)(lambda: weights_do(lambda c: c.wait_send(), (1, 2, 3)))

    passes = ((1, 1), (0, 3))

    @pl.when(works)
    def _():
        for k, d in passes:
            @pl.when(needed[k] & (peers[d] < SA - 1))
            def _():
                own_copy(k, peers[d]).wait()
                pass_on(k, d).start()
        for d in range(SA):
            for k in (1, 0):
                if (k, d) not in passes:
                    @pl.when(needed[k] & (peers[d] < SA - 1))
                    def _():
                        own_copy(k, peers[d]).wait()
        pl.when((sa == SA - 1) & ((gx >= nx - 2) | (z >= 5)))(send_interior)

    needed_m = (gx >= 0, has_south)

    def do_native():
        @pl.when(has_south)
        def _():
            south_copy.wait_recv()
            unpack(south, traces, NS + NT)
        pl.when(jnp.logical_not(has_south))(lambda: clear(traces, NS + NT))
        @pl.when(has_west)
        def _():
            west_copy.wait_recv()
            unpack(west, traces, NS)
        pl.when(jnp.logical_not(has_west))(lambda: clear(traces, NS))
        for base, ref in ((NT, north), (0, east)):
            for o in range(base, base + NT, 2):
                both = jnp.concatenate([row(o), row(o + 1)], axis=0)
                ref[(o - base) * N:(o - base + 2) * N, :] = both.astype(jnp.bfloat16)
            if base:
                pl.when(has_north)(lambda: south_copy.start())

        @pl.when(before_end)
        def _():
            pl.semaphore_wait(ack_sem, 1)
            west_end_copy.start()

    @pl.when(host)
    def _():
        @pl.when(jnp.logical_not(has_south))
        def _():
            for p in range(SA):
                moved[1][p] = jnp.zeros((SENT[1], BLK, BLK), jnp.bfloat16)
        for k, h in CHUNKS:
            @pl.when(needed_m[k])
            def _():
                def move_on(last):
                    moved_copy(k, h, sa, peers[1], last).wait_recv()
                    for d in (1, 3):
                        moved_copy(k, h, sa, peers[d], last).start()
                each(sa, move_on)
        for k, h in CHUNKS:
            @pl.when(needed_m[k])
            def _():
                def move_on(last):
                    moved_copy(k, h, peers[1 if h else SA - 1], sa, last).wait_recv()
                    pass_moved(k, h, last).start()
                each(peers[1 if h else SA - 1], move_on)
        cols_move.wait_recv()
        to_smem = pltpu.make_async_copy(cols_vmem, cols_m, local_sem)
        to_smem.start()
        to_smem.wait()
        part_move.wait_recv()
        for k, h in CHUNKS:
            @pl.when(needed_m[k])
            def _():
                for d in (SA - 1 if h else 1, 2):
                    each(peers[d], lambda last: moved_copy(k, h, peers[d], sa, last).wait_recv())

    pl.when(works)(do_native)

    @pl.when(host)
    def _():
        unpack(east, traces_m, NS)

        @pl.when(has_south)
        def _():
            south_m_copy.wait_recv()
            unpack(south_m, traces_m, NS + NT)
        pl.when(jnp.logical_not(has_south))(lambda: clear(traces_m, NS + NT))
        for base, ref in ((NT, north_m), (0, east_m)):
            for o in range(base, base + NT, 2):
                both = jnp.concatenate([row_m(o), row_m(o + 1)], axis=0)
                both = (both + part_m[o * N:(o + 2) * N, :].astype(jnp.float32)).astype(jnp.bfloat16)
                ref[(o - base) * N:(o - base + 2) * N, :] = both
            if base:
                pl.when(has_north)(lambda: south_m_copy.start())
        west_copy.start()
        back_west.start()
        pl.when(has_south)(lambda: back_south.start())
        back_east.start()
        back_north.start()
        pl.when((sa == SA - 1) & (z < 5))(send_interior)

    @pl.when(works)
    def _():
        arrived(SA - 1)
        interior()
        put_out()
        pl.when(sa < SA - 1)(lambda: weights_do(lambda c: c.wait_send(), (1, 3)))
        pl.when(sa == SA - 1)(lambda: weights_do(lambda c: c.wait_send(), (1, 2, 3)))
        for k, d in passes:
            pl.when(needed[k] & (peers[d] < SA - 1))(lambda: pass_on(k, d).wait_send())
        pl.when(has_north)(lambda: south_copy.wait_send())
        pl.when(before_end)(lambda: west_end_copy.wait_send())

        @pl.when(host)
        def _():
            for k, h in CHUNKS:
                @pl.when(needed_m[k])
                def _():
                    for d in (1, 3):
                        each(sa, lambda last: moved_copy(k, h, sa, peers[d], last).wait_send())
                    each(peers[1 if h else SA - 1], lambda last: pass_moved(k, h, last).wait_send())
            pl.when(has_north)(lambda: south_m_copy.wait_send())
            west_copy.wait_send()
            back_west.wait_send()
            pl.when(has_south)(lambda: back_south.wait_send())
            back_east.wait_send()
            back_north.wait_send()

    for d in (1, 2, 3):
        scaled_copy(sa, peers[d]).wait_send()
        part_copy(sa, peers[d]).wait_send()


def on_device(nx, ny, source, group_gain, shot_group, block_cols, block_vals):
    vmem, smem, hbm = (pl.BlockSpec(memory_space=m) for m in (pltpu.VMEM, pltpu.SMEM, pl.ANY))
    dma = pltpu.SemaphoreType.DMA
    bf16, f32 = jnp.bfloat16, jnp.float32
    trace = pltpu.VMEM((NT * N, BLK), bf16)
    cols = block_cols[0, 0].T
    outs = pl.pallas_call(
        functools.partial(kernel, nx, ny),
        out_shape=[jax.ShapeDtypeStruct((N, NT * BLK), bf16), jax.ShapeDtypeStruct((N, NT * BLK), bf16),
                   jax.ShapeDtypeStruct((N, (OUTB - TRACED) * BLK), bf16)],
        in_specs=[vmem, smem, smem, smem, hbm, hbm],
        out_specs=[vmem, vmem, vmem],
        scratch_shapes=[
            pltpu.VMEM((OUTB, 2, BLK, BLK), bf16),
            pltpu.VMEM((OWN, 4, BLK, BLK), bf16),
            pltpu.VMEM((SA, NS * N, BLK), bf16),
            pltpu.VMEM((NS, SA * N, BLK), f32),
            pltpu.VMEM((SA, OWN, N, BLK), f32),
            pltpu.VMEM((SA, OWN, N, BLK), f32),
            pltpu.VMEM((NS + 2 * NT, N, BLK), f32),
            trace, trace, trace, trace,
            *[pltpu.VMEM((SA, sent, BLK, BLK), bf16) for sent in SENT],
            *[pltpu.VMEM(((SA - 1) * lot, BLK, BLK), bf16) for lot in LOT],
            pltpu.VMEM((TRACED * N, BLK), bf16),
            pltpu.VMEM((TRACED * N, BLK), bf16),
            pltpu.VMEM(cols.shape, jnp.int32),
            pltpu.SMEM(cols.shape, jnp.int32),
            pltpu.VMEM((NS + 2 * NT, N, BLK), f32),
            trace, trace, trace,
            dma, dma((2, SA)), dma((2, SA)), dma((SA,)), dma((SA,)), dma((SA,)), dma((SA,)), dma((7,)), dma((5,)),
            dma((2,)), dma((2, SA - 1)), dma((2, 2)), dma((2,)), dma((2,)), dma((2, 2, SA)), dma((2, 2, SA)), dma((2,)), dma((2, 2)),
            pltpu.SemaphoreType.REGULAR, pltpu.SemaphoreType.REGULAR,
        ],
        compiler_params=pltpu.CompilerParams(collective_id=0, has_side_effects=True, vmem_limit_bytes=107 << 19),
        name="sweep",
    )(source[0, 0], group_gain, shot_group, cols, cols, block_vals[0, 0])
    return tuple(out[None, None] for out in outs)


def solution(mesh):
    placed = (
        P("gx", "gy", "sa", None),
        P(),
        P("sa"),
        P("gx", "gy", None, None),
        P("gx", "gy", "sa", None, None, None),
    )
    return jax.shard_map(
        functools.partial(on_device, mesh.shape["gx"], mesh.shape["gy"]),
        mesh=mesh,
        in_specs=placed,
        out_specs=(P("gx", "gy", "sa", None), P("gx", "gy", "sa", None), P("gx", "gy", "sa", None)),
        check_vma=False,
    )
```

```python
import functools

import jax
import jax.numpy as jnp
from jax import lax
from jax.experimental import pallas as pl
from jax.experimental.pallas import tpu as pltpu
from jax.sharding import PartitionSpec as P

MESH = pl.DeviceIdType.MESH
BLK = 128
NT = 12
NS = 6
OUTB = 32
SA = 4
OWN = OUTB // SA
N = 8
TRACED = 2 * NT
CHUNKS = ((0, 0), (0, 1), (1, 0), (1, 1))
SENT = (6, 7)
LOT = tuple(OWN - sent for sent in SENT)


STEP = 2


def piece(k, h, last):
    count = (SA - 1) * LOT[k] if last else SENT[k]
    first = (count + 1) // 2
    return pl.ds(first, count - first) if h else pl.ds(0, first)


def sent_slot(o, k):
    owner, r = divmod(o, OWN)
    return (owner, r) if r < SENT[k] else (SA - 1, LOT[k] * owner + r - SENT[k])


def each(owner, act):
    pl.when(owner < SA - 1)(lambda: act(False))
    pl.when(owner == SA - 1)(lambda: act(True))


def kernel(nx, ny, source, gain, group, cols, cols_hbm, vals_hbm, east_out, north_out, inner_out,
           weights, vals, scaled_all, picked_src, part_send, part, traces, west, south, east, north,
           moved_w, moved_s, stage_w, stage_s, part_moved, part_m, cols_vmem, cols_m, traces_m, south_m, east_m, north_m,
           local_sem, w_send, w_recv, s_send, s_recv, p_send, p_recv, t_send, t_recv,
           h_send, h_recv, z_send, z_more, e_recv, m_send, m_recv, f_send, f_moved, go_sem, ack_sem):
    gx, gy, sa = lax.axis_index("gx"), lax.axis_index("gy"), lax.axis_index("sa")
    moved, stage = (moved_w, moved_s), (stage_w, stage_s)
    odd = lax.rem(gx, 2)
    z = gy // 2
    peers = [lax.rem(sa + d, SA) for d in range(SA)]
    donor = (odd == 1) & (gx < nx - 1)
    host = (odd == 0) & (gx < nx - 2)
    works = jnp.logical_not(donor)
    ends = gx == nx - 1
    before_end = gx == nx - 2
    has_west, has_south, has_north = gx > 0, gy > 0, gy < ny - 1
    z_odd = lax.rem(z, 2) == 1
    chained = donor & z_odd
    chains = chained & (gy < ny - 4)

    barrier = pltpu.get_barrier_semaphore()
    near = (
        ((odd == 0) & (gx < nx - 2), 2, 0), ((odd == 0) & (gx > 1), -2, 0),
        (works & has_south, 0, -1), (works & has_north, 0, 1),
        (chained & (gy >= 4), 0, -4), (chains, 0, 4),
    )
    for there, dx, dy in ((odd == 0, 1, 0),) + near:
        @pl.when(there)
        def _():
            pl.semaphore_signal(barrier, inc=1, device_id=(gx + dx, gy + dy, sa), device_id_type=MESH)
    for d in range(1, SA):
        pl.semaphore_signal(barrier, inc=1, device_id=(gx, gy, peers[d]), device_id_type=MESH)

    load = pltpu.make_async_copy(vals_hbm, vals, local_sem)
    load.start()

    shot = lax.broadcasted_iota(jnp.int32, (N, BLK), 0)
    gains = jnp.zeros((N, BLK), jnp.float32)
    for s in range(N):
        gains = jnp.where(shot == s, gain[group[s]], gains)
    for pair in range(NS // 2):
        halves = [source[:, (2 * pair + h) * BLK:(2 * pair + h + 1) * BLK].astype(jnp.float32) * gains for h in (0, 1)]
        scaled_all[sa, pair * 16:(pair + 1) * 16, :] = jnp.concatenate(halves, axis=0).astype(jnp.bfloat16)

    load.wait()
    pl.semaphore_wait(barrier, 3 + odd + sum(there.astype(jnp.int32) for there, _, _ in near))

    def copy(src, dst, send, recv, dx=0, dy=0, to=None):
        return pltpu.make_async_remote_copy(src, dst, send, recv, device_id=(gx + dx, gy + dy, sa if to is None else to),
                                            device_id_type=MESH)

    def scaled_copy(owner, peer):
        return copy(scaled_all.at[owner], scaled_all.at[owner], s_send.at[peer], s_recv.at[owner], to=peer)

    def part_copy(owner, peer):
        return copy(part_send.at[peer], part.at[owner], p_send.at[peer], p_recv.at[owner], to=peer)

    def weight_copy(k, owner, peer):
        rows = pl.ds(owner * OWN, OWN)
        return copy(vals.at[:, k:k + 1], weights.at[rows, k:k + 1], w_send.at[k, peer], w_recv.at[k, owner], to=peer)

    def own_copy(k, p):
        rows = pl.ds(p * OWN, OWN)
        return pltpu.make_async_copy(vals.at[:, k:k + 1], weights.at[rows, k:k + 1], w_recv.at[k, p])

    needed = (has_west, has_south)

    def weights_do(act, ds):
        for k in (1, 0):
            @pl.when(needed[k])
            def _():
                for d in ds:
                    act(weight_copy(k, sa, peers[d]))

    def send_interior():
        weights_do(lambda c: c.start(), (2, 1, 3))

    def arrived(p):
        for k in (1, 0):
            @pl.when(needed[k])
            def _():
                own_copy(k, p).wait()

    def pass_on(k, d):
        rows = pl.ds(peers[d] * OWN, OWN)
        ref = weights.at[rows, k:k + 1]
        return copy(ref, ref, f_send.at[k], w_recv.at[k, peers[d]], to=peers[SA - d])

    def pass_moved(k, h, last):
        d = 1 if h else SA - 1
        ref = moved[k].at[peers[d], piece(k, h, last)]
        return copy(ref, ref, f_moved.at[k, h], m_recv.at[k, h, peers[d]], to=peers[SA - d])

    def shuffle_copy(k, owner):
        return copy(vals.at[pl.ds(SENT[k], LOT[k]), k], stage[k].at[pl.ds(owner * LOT[k], LOT[k])], h_send.at[k],
                    h_recv.at[k, owner], to=SA - 1)

    def move_copy(k, h, last):
        rows = piece(k, h, last)
        src = stage[k].at[rows] if last else vals.at[rows, k]
        return copy(src, moved[k].at[sa, rows], z_send.at[k, h], m_recv.at[k, h, sa], dx=-1)

    def moved_copy(k, h, owner, peer, last):
        ref = moved[k].at[owner, piece(k, h, last)]
        return copy(ref, ref, m_send.at[k, h, peer], m_recv.at[k, h, owner], to=peer)

    part_move = copy(part_moved, part_m, z_more.at[0], e_recv.at[0], dx=-1)
    cols_move = copy(cols_hbm, cols_vmem, z_more.at[1], e_recv.at[1], dx=-1)

    def moves(act, chunks):
        for last in (False, True):
            @pl.when((sa == SA - 1) if last else (sa < SA - 1))
            def _():
                for k, h in chunks:
                    pl.when(needed[k])(lambda: act(move_copy(k, h, last)))

    gated = jnp.logical_not(z_odd) & (z >= 4)

    def start_moves():
        pl.when(jnp.logical_not(gated))(lambda: moves(lambda c: c.start(), CHUNKS))

        @pl.when(gated)
        def _():
            for k, h in CHUNKS:
                def bit_by_bit(last):
                    src = stage[k] if last else vals.at[:, k]
                    rows = piece(k, h, last)
                    for r in range(rows.start, rows.start + rows.size, STEP):
                        some = pl.ds(r, min(STEP, rows.start + rows.size - r))
                        c = copy(src.at[some], moved[k].at[sa, some], z_send.at[k, h], m_recv.at[k, h, sa], dx=-1)
                        c.start()
                        c.wait_send()
                pl.when(needed[k])(lambda: each(sa, bit_by_bit))

    early = donor & (jnp.logical_not(z_odd) | (z == 1))
    late = donor & z_odd & (z > 1)

    @pl.when(donor & (sa < SA - 1))
    def _():
        for k in (0, 1):
            shuffle_copy(k, sa).start()
    pl.when(donor)(lambda: cols_move.start())
    pl.when(early & (sa < SA - 1))(start_moves)
    for d in (2, 1, 3):
        scaled_copy(sa, peers[d]).start()
    pl.when(ends)(lambda: pl.semaphore_signal(ack_sem, inc=1, device_id=(gx - 1, gy, sa), device_id_type=MESH))

    @pl.when(donor & (sa == SA - 1))
    def _():
        for owner in range(SA - 1):
            for k in (0, 1):
                shuffle_copy(k, owner).wait_recv()
        pl.when(early)(start_moves)

    for d in (1, 3, 2):
        scaled_copy(peers[d], peers[d]).wait_recv()
    for p in range(SA):
        for pair in range(NS // 2):
            both = scaled_all[p, pair * 16:(pair + 1) * 16, :].astype(jnp.float32)
            picked_src[2 * pair, p * N:(p + 1) * N, :] = both[:N]
            picked_src[2 * pair + 1, p * N:(p + 1) * N, :] = both[N:]
    for r in range(OWN):
        o = sa * OWN + r
        left = jnp.concatenate([picked_src[cols[2, o]], picked_src[cols[3, o]]], axis=1).astype(jnp.bfloat16)
        out = jnp.dot(left, vals[r, 2:4].reshape(2 * BLK, BLK), preferred_element_type=jnp.float32)
        for p in range(SA):
            part_send[p, r] = out[p * N:(p + 1) * N]
    for d in (2, 1, 3):
        part_copy(sa, peers[d]).start()

    pl.when(works & (sa < SA - 1))(lambda: weights_do(lambda c: c.start(), (1, 3)))
    gathers = works | (sa == SA - 1)
    for k in (1, 0):
        @pl.when(needed[k] & gathers)
        def _():
            own_copy(k, sa).start()

        @pl.when(jnp.logical_not(needed[k]))
        def _():
            weights[:, k] = jnp.zeros((OUTB, BLK, BLK), jnp.bfloat16)
    part[sa] = part_send[sa]
    for d in (1, 3, 2):
        part_copy(peers[d], peers[d]).wait_recv()

    def unpack(ref, dst, base):
        for pair in range(NT // 2):
            both = ref[pair * 16:(pair + 1) * 16, :].astype(jnp.float32)
            dst[base + 2 * pair] = both[:N]
            dst[base + 2 * pair + 1] = both[N:]

    def clear(dst, base):
        for b in range(NT):
            dst[base + b] = jnp.zeros((N, BLK), jnp.float32)

    def row(o):
        left = jnp.concatenate([traces[cols[0, o]], traces[cols[1, o]]], axis=1).astype(jnp.bfloat16)
        out = jnp.dot(left, weights[o].reshape(2 * BLK, BLK), preferred_element_type=jnp.float32)
        return out + part[o // OWN, o % OWN]

    def row_m(o):
        left = jnp.concatenate([traces_m[cols_m[0, o]], traces_m[cols_m[1, o]]], axis=1).astype(jnp.bfloat16)
        blocks = jnp.concatenate([moved[k][sent_slot(o, k)] for k in (0, 1)], axis=0)
        return jnp.dot(left, blocks, preferred_element_type=jnp.float32)

    def interior():
        for o in range(TRACED, OUTB):
            inner_out[:, (o - TRACED) * BLK:(o - TRACED + 1) * BLK] = row(o).astype(jnp.bfloat16)

    def put_out():
        for ref, out in ((east, east_out), (north, north_out)):
            for pair in range(NT // 2):
                both = ref[pair * 16:(pair + 1) * 16, :]
                out[:, 2 * pair * BLK:(2 * pair + 1) * BLK] = both[:N]
                out[:, (2 * pair + 1) * BLK:(2 * pair + 2) * BLK] = both[N:]

    west_copy = copy(east_m, west, t_send.at[0], t_recv.at[0], dx=2)
    west_end_copy = copy(east, west, t_send.at[0], t_recv.at[0], dx=1)
    south_copy = copy(north, south, t_send.at[1], t_recv.at[1], dy=1)
    south_m_copy = copy(north_m, south_m, t_send.at[2], t_recv.at[2], dy=1)
    back_west = copy(east, west, t_send.at[3], t_recv.at[0], dx=1)
    back_south = copy(south_m, south, t_send.at[4], t_recv.at[1], dx=1)
    back_east = copy(east_m, east, t_send.at[5], t_recv.at[3], dx=1)
    back_north = copy(north_m, north, t_send.at[6], t_recv.at[4], dx=1)

    @pl.when(donor)
    def _():
        for o in range(0, TRACED, 2):
            both = jnp.concatenate([part[o // OWN, o % OWN], part[o // OWN, o % OWN + 1]], axis=0)
            part_moved[o * N:(o + 2) * N, :] = both.astype(jnp.bfloat16)

        @pl.when(late)
        def _():
            pl.semaphore_wait(go_sem, 1)
            start_moves()
        part_move.start()
        pl.when(jnp.logical_not(gated))(lambda: moves(lambda c: c.wait_send(), CHUNKS))

        @pl.when(chains)
        def _():
            pl.semaphore_signal(go_sem, inc=1, device_id=(gx, gy + 4, sa), device_id_type=MESH)
        part_move.wait_send()
        pl.when(sa == SA - 1)(send_interior)
        arrived(SA - 1)
        back_west.wait_recv()
        unpack(west, traces, NS)

        @pl.when(has_south)
        def _():
            back_south.wait_recv()
            unpack(south, traces, NS + NT)
        pl.when(jnp.logical_not(has_south))(lambda: clear(traces, NS + NT))
        interior()
        back_east.wait_recv()
        back_north.wait_recv()
        put_out()
        cols_move.wait_send()
        for k in (0, 1):
            pl.when(sa < SA - 1)(lambda: shuffle_copy(k, sa).wait_send())

        pl.when(sa == SA - 1)(lambda: weights_do(lambda c: c.wait_send(), (1, 2, 3)))

    passes = ((1, 1), (0, 3))

    @pl.when(works)
    def _():
        for k, d in passes:
            @pl.when(needed[k] & (peers[d] < SA - 1))
            def _():
                own_copy(k, peers[d]).wait()
                pass_on(k, d).start()
        for d in range(SA):
            for k in (1, 0):
                if (k, d) not in passes:
                    @pl.when(needed[k] & (peers[d] < SA - 1))
                    def _():
                        own_copy(k, peers[d]).wait()
        pl.when((sa == SA - 1) & ((gx >= nx - 2) | (z >= 4)))(send_interior)

    needed_m = (gx >= 0, has_south)

    def do_native():
        @pl.when(has_south)
        def _():
            south_copy.wait_recv()
            unpack(south, traces, NS + NT)
        pl.when(jnp.logical_not(has_south))(lambda: clear(traces, NS + NT))
        @pl.when(has_west)
        def _():
            west_copy.wait_recv()
            unpack(west, traces, NS)
        pl.when(jnp.logical_not(has_west))(lambda: clear(traces, NS))
        for base, ref in ((NT, north), (0, east)):
            for o in range(base, base + NT, 2):
                both = jnp.concatenate([row(o), row(o + 1)], axis=0)
                ref[(o - base) * N:(o - base + 2) * N, :] = both.astype(jnp.bfloat16)
            if base:
                pl.when(has_north)(lambda: south_copy.start())

        @pl.when(before_end)
        def _():
            pl.semaphore_wait(ack_sem, 1)
            west_end_copy.start()

    @pl.when(host)
    def _():
        @pl.when(jnp.logical_not(has_south))
        def _():
            for p in range(SA):
                moved[1][p] = jnp.zeros((SENT[1], BLK, BLK), jnp.bfloat16)
        for k, h in CHUNKS:
            @pl.when(needed_m[k])
            def _():
                def move_on(last):
                    moved_copy(k, h, sa, peers[1], last).wait_recv()
                    for d in (1, 3):
                        moved_copy(k, h, sa, peers[d], last).start()
                each(sa, move_on)
        for k, h in CHUNKS:
            @pl.when(needed_m[k])
            def _():
                def move_on(last):
                    moved_copy(k, h, peers[1 if h else SA - 1], sa, last).wait_recv()
                    pass_moved(k, h, last).start()
                each(peers[1 if h else SA - 1], move_on)
        cols_move.wait_recv()
        to_smem = pltpu.make_async_copy(cols_vmem, cols_m, local_sem)
        to_smem.start()
        to_smem.wait()
        part_move.wait_recv()
        for k, h in CHUNKS:
            @pl.when(needed_m[k])
            def _():
                for d in (SA - 1 if h else 1, 2):
                    each(peers[d], lambda last: moved_copy(k, h, peers[d], sa, last).wait_recv())

    pl.when(works)(do_native)

    @pl.when(host)
    def _():
        unpack(east, traces_m, NS)

        @pl.when(has_south)
        def _():
            south_m_copy.wait_recv()
            unpack(south_m, traces_m, NS + NT)
        pl.when(jnp.logical_not(has_south))(lambda: clear(traces_m, NS + NT))
        for base, ref in ((NT, north_m), (0, east_m)):
            for o in range(base, base + NT, 2):
                both = jnp.concatenate([row_m(o), row_m(o + 1)], axis=0)
                both = (both + part_m[o * N:(o + 2) * N, :].astype(jnp.float32)).astype(jnp.bfloat16)
                ref[(o - base) * N:(o - base + 2) * N, :] = both
            if base:
                pl.when(has_north)(lambda: south_m_copy.start())
        west_copy.start()
        back_west.start()
        pl.when(has_south)(lambda: back_south.start())
        back_east.start()
        back_north.start()
        pl.when((sa == SA - 1) & (z < 4))(send_interior)

    @pl.when(works)
    def _():
        arrived(SA - 1)
        interior()
        put_out()
        pl.when(sa < SA - 1)(lambda: weights_do(lambda c: c.wait_send(), (1, 3)))
        pl.when(sa == SA - 1)(lambda: weights_do(lambda c: c.wait_send(), (1, 2, 3)))
        for k, d in passes:
            pl.when(needed[k] & (peers[d] < SA - 1))(lambda: pass_on(k, d).wait_send())
        pl.when(has_north)(lambda: south_copy.wait_send())
        pl.when(before_end)(lambda: west_end_copy.wait_send())

        @pl.when(host)
        def _():
            for k, h in CHUNKS:
                @pl.when(needed_m[k])
                def _():
                    for d in (1, 3):
                        each(sa, lambda last: moved_copy(k, h, sa, peers[d], last).wait_send())
                    each(peers[1 if h else SA - 1], lambda last: pass_moved(k, h, last).wait_send())
            pl.when(has_north)(lambda: south_m_copy.wait_send())
            west_copy.wait_send()
            back_west.wait_send()
            pl.when(has_south)(lambda: back_south.wait_send())
            back_east.wait_send()
            back_north.wait_send()

    for d in (1, 2, 3):
        scaled_copy(sa, peers[d]).wait_send()
        part_copy(sa, peers[d]).wait_send()


def on_device(nx, ny, source, group_gain, shot_group, block_cols, block_vals):
    vmem, smem, hbm = (pl.BlockSpec(memory_space=m) for m in (pltpu.VMEM, pltpu.SMEM, pl.ANY))
    dma = pltpu.SemaphoreType.DMA
    bf16, f32 = jnp.bfloat16, jnp.float32
    trace = pltpu.VMEM((NT * N, BLK), bf16)
    cols = block_cols[0, 0].T
    outs = pl.pallas_call(
        functools.partial(kernel, nx, ny),
        out_shape=[jax.ShapeDtypeStruct((N, NT * BLK), bf16), jax.ShapeDtypeStruct((N, NT * BLK), bf16),
                   jax.ShapeDtypeStruct((N, (OUTB - TRACED) * BLK), bf16)],
        in_specs=[vmem, smem, smem, smem, hbm, hbm],
        out_specs=[vmem, vmem, vmem],
        scratch_shapes=[
            pltpu.VMEM((OUTB, 2, BLK, BLK), bf16),
            pltpu.VMEM((OWN, 4, BLK, BLK), bf16),
            pltpu.VMEM((SA, NS * N, BLK), bf16),
            pltpu.VMEM((NS, SA * N, BLK), f32),
            pltpu.VMEM((SA, OWN, N, BLK), f32),
            pltpu.VMEM((SA, OWN, N, BLK), f32),
            pltpu.VMEM((NS + 2 * NT, N, BLK), f32),
            trace, trace, trace, trace,
            *[pltpu.VMEM((SA, sent, BLK, BLK), bf16) for sent in SENT],
            *[pltpu.VMEM(((SA - 1) * lot, BLK, BLK), bf16) for lot in LOT],
            pltpu.VMEM((TRACED * N, BLK), bf16),
            pltpu.VMEM((TRACED * N, BLK), bf16),
            pltpu.VMEM(cols.shape, jnp.int32),
            pltpu.SMEM(cols.shape, jnp.int32),
            pltpu.VMEM((NS + 2 * NT, N, BLK), f32),
            trace, trace, trace,
            dma, dma((2, SA)), dma((2, SA)), dma((SA,)), dma((SA,)), dma((SA,)), dma((SA,)), dma((7,)), dma((5,)),
            dma((2,)), dma((2, SA - 1)), dma((2, 2)), dma((2,)), dma((2,)), dma((2, 2, SA)), dma((2, 2, SA)), dma((2,)), dma((2, 2)),
            pltpu.SemaphoreType.REGULAR, pltpu.SemaphoreType.REGULAR,
        ],
        compiler_params=pltpu.CompilerParams(collective_id=0, has_side_effects=True, vmem_limit_bytes=107 << 19),
        name="sweep",
    )(source[0, 0], group_gain, shot_group, cols, cols, block_vals[0, 0])
    return tuple(out[None, None] for out in outs)


def solution(mesh):
    placed = (
        P("gx", "gy", "sa", None),
        P(),
        P("sa"),
        P("gx", "gy", None, None),
        P("gx", "gy", "sa", None, None, None),
    )
    return jax.shard_map(
        functools.partial(on_device, mesh.shape["gx"], mesh.shape["gy"]),
        mesh=mesh,
        in_specs=placed,
        out_specs=(P("gx", "gy", "sa", None), P("gx", "gy", "sa", None), P("gx", "gy", "sa", None)),
        check_vma=False,
    )
```
